32 devices in a mesh: groups: 2 (over y), dp: 4 (over x, core), fsdp: 4 (over z).
Axes of the slice: x: 2, y: 2, z: 4, core: 2. Of those that a mesh axis runs over, the one named last changes fastest.
Arguments:
- input_rows: bfloat16 [2560, 6144], P(('groups', 'dp'), 'fsdp'), parts along dimension 0, may hold values from -6 to 6
- cotangent: bfloat16 [1280, 16384], P(('groups', 'dp'), 'fsdp'), parts along dimension 0, may hold values from -1.5 to 1.5
- frozen_weight: bfloat16 [6144, 16384], P(None, 'fsdp'), may hold values from -0.078125 to 0.078125
- adapter_down_weight: bfloat16 [64, 6144, 64], P('groups', 'fsdp'), parts along dimension 0, may hold values from -0.078125 to 0.078125
- adapter_up_weight: bfloat16 [64, 64, 16384], P('groups', None, 'fsdp'), parts along dimension 0, may hold values from -0.75 to 0.75
- tenant_row_counts: int32 [8, 32], P('groups'), parts along dimension 0, may hold values from 0 to 160, as said below
- handoff_counts: int32 [8, 4], P('groups'), parts along dimension 0, may hold values from 0 to 160, as said below
- tenant_gradient_slot: int32 [64], P('groups'), parts along dimension 0, may hold values from 0 to 31, each once
Outputs:
- outputs: bfloat16 [1280, 16384], P(('groups', 'dp'), 'fsdp'), parts along dimension 0
- row_grad: bfloat16 [2560, 6144], P(('groups', 'dp'), 'fsdp'), parts along dimension 0
- grad_a: bfloat16 [64, 6144, 64], P(('groups', 'dp'), 'fsdp'), parts along dimension 0
- grad_b: bfloat16 [64, 64, 16384], P(('groups', 'dp'), None, 'fsdp'), parts along dimension 0
The draws below stay inside these ranges and needn't reach their ends.
There are 2 independent parts, one for each index of `groups`. The reference program is written for one: setup_inputs(seed, part) draws one part's arguments, and reference() takes and returns one part's arrays. A program takes and returns all parts, laid end to end along the dimension named above; an argument that names none is the same for every part. Nothing has to cross between parts.
Inputs may be any that keep to these rules, and one draw needn't show every extreme that they name: A group's rows of input_rows are its first (sum of its row of tenant_row_counts) rows, tenant 0's first, then tenant 1's and so on; the other rows are unused. One group holds 320 rows in every draw, and one tenant of that group holds exactly 160 of them. `handoff_counts`: row i sums to group i's rows (the sum of row i of tenant_row_counts); every column sums to 160. Group i hands its rows out in order: the first S[i, 0] to group 0, the next S[i, 1] to group 1, and so on (the diagonal entry counts the rows it keeps). Off the diagonal an entry is at most 80, and some entry reaches it in every draw; some diagonal entry is 160 in every draw. `tenant_gradient_slot`: each slot once; slot s belongs to data group s // 8.
All inputs are finite; a program needn't handle non-finite values.
Results may differ from the reference program's by a relative error of at most 0.01.
Values may be sent and summed in bfloat16 or wider, within the bound.
No kernel may reach another device: no remote copies, remote signals or barrier semaphores. Data moves between devices by JAX's collectives and lax.ppermute only.
A program may use at most 256 MiB of HBM per device.

```python
import jax
import jax.numpy as jnp
from jax import lax

MODEL_WIDTH = 6144
HIDDEN_UNITS = 16384
ADAPTER_RANK = 64
TENANT_COUNT = 32
TOK_GRP = 160
TOKENS = 640
ROWS_IN = 1280
N_DP = 4


def group_plan(key):
    order = jax.random.permutation(jax.random.fold_in(key, 11), N_DP)
    split = jax.random.randint(jax.random.fold_in(key, 12), (), TOK_GRP // 8, 3 * TOK_GRP // 8 + 1)
    by_rank = jnp.array([0, TOK_GRP // 2, 0, TOK_GRP // 2], jnp.int32) + jnp.array([0, 0, 1, -1], jnp.int32) * split
    moved = jnp.zeros((N_DP,), jnp.int32).at[order].set(by_rank)
    heavy = (jnp.arange(N_DP) == order[0]).astype(jnp.int32)
    keeps = heavy * TOK_GRP + (1 - heavy) * (TOK_GRP - moved)
    return (jnp.diag(keeps) + heavy[:, None] * moved[None, :]).astype(jnp.int32)


def draw_handoff_counts(key, part):
    plan = group_plan(key)
    return plan


def draw_tenant_row_counts(key, part):
    loads = jnp.sum(group_plan(key), axis=1).astype(jnp.int32)
    key = jax.random.fold_in(key, 5)
    chosen = jax.random.randint(jax.random.fold_in(key, 7), (), 0, TENANT_COUNT).astype(jnp.int32)
    column_index = jnp.arange(TENANT_COUNT, dtype=jnp.int32)
    full = (loads == 2 * TOK_GRP).astype(jnp.int32)
    held = (column_index == chosen).astype(jnp.int32)
    weights = jax.random.randint(key, (N_DP, TENANT_COUNT), 1, 17)
    weights = weights * (1 - full[:, None] * held[None, :])
    rest_loads = loads - full * TOK_GRP
    shares = rest_loads[:, None] * weights // jnp.sum(weights, axis=1, keepdims=True)
    rest = rest_loads - jnp.sum(shares, axis=1)
    after = (column_index == (chosen + 1) % TENANT_COUNT).astype(jnp.int32)
    counts = shares + rest[:, None] * after[None, :] + full[:, None] * held[None, :] * TOK_GRP
    return counts.astype(jnp.int32)


def shard_levels(own_key, shape, cuts, low, high):
    loudness, own = 1.0, jax.random.fold_in(own_key, 6)
    for position, blocks in cuts:
        heights = jnp.exp(jax.random.uniform(jax.random.fold_in(own, position), (blocks,), jnp.float32, low / len(cuts), high / len(cuts)))
        loudness = loudness * jnp.repeat(heights, shape[position] // blocks).reshape([-1 if axis == position else 1 for axis in range(len(shape))])
    return loudness


def centred(rng, extent, deviation, bound, shards=(), held_as=jnp.bfloat16):
    gain = shard_levels(rng, extent, shards, -0.22, 0.18) if shards else 1.0
    values = jax.random.normal(rng, extent, jnp.float32) * deviation * gain
    return jnp.minimum(jnp.maximum(values, -bound), bound).astype(held_as)


def setup_inputs(seed: int = 0, part: int = 0) -> dict:
    streams_of = jax.random.split(jax.random.key(seed), 9)
    own_keys = jax.random.split(jax.random.fold_in(streams_of[8], part), 9)
    return {
        "input_rows": centred(own_keys[0], (ROWS_IN, MODEL_WIDTH), 1.0, 6.0, ((0, 4), (1, 4))),
        "cotangent": centred(own_keys[1], (TOKENS, HIDDEN_UNITS), 0.25, 1.5, ((0, 4), (1, 4))),
        "frozen_weight": centred(streams_of[2], (MODEL_WIDTH, HIDDEN_UNITS), MODEL_WIDTH ** -0.5, 0.078125, ((1, 4),)),
        "adapter_down_weight": centred(own_keys[3], (TENANT_COUNT, MODEL_WIDTH, ADAPTER_RANK), MODEL_WIDTH ** -0.5, 0.078125, ((1, 4),)),
        "adapter_up_weight": centred(own_keys[4], (TENANT_COUNT, ADAPTER_RANK, HIDDEN_UNITS), ADAPTER_RANK ** -0.5, 0.75, ((2, 4),)),
        "tenant_row_counts": draw_tenant_row_counts(jax.random.fold_in(jax.random.fold_in(streams_of[8], part), 71), part),
        "handoff_counts": draw_handoff_counts(jax.random.fold_in(jax.random.fold_in(streams_of[8], part), 71), part),
        "tenant_gradient_slot": jax.random.permutation(own_keys[7], TENANT_COUNT).astype(jnp.int32),
    }


adapter_scale = 0.25


def balanced_sources(handoff_counts, balanced_rows):
    groups = handoff_counts.shape[0]
    sent_before = (jnp.cumsum(handoff_counts, axis=1) - handoff_counts).astype(jnp.int32)
    recv_before = (jnp.cumsum(handoff_counts, axis=0) - handoff_counts).astype(jnp.int32)
    target = jnp.arange(groups * balanced_rows, dtype=jnp.int32)
    destination = (target // balanced_rows).astype(jnp.int32)
    places = (target % balanced_rows).astype(jnp.int32)
    starts = jnp.take(recv_before, destination, axis=1).T
    counts = jnp.take(handoff_counts, destination, axis=1).T
    inside = (places[:, None] >= starts) & (places[:, None] < starts + counts)
    numbers = jnp.arange(groups, dtype=jnp.int32)[None, :]
    source = jnp.sum(jnp.where(inside, numbers, 0), axis=1).astype(jnp.int32)
    offset = (places - jnp.sum(jnp.where(inside, starts, 0), axis=1)).astype(jnp.int32)
    source_row = (sent_before[source, destination] + offset).astype(jnp.int32)
    return source, source_row


def reference(input_rows, cotangent, frozen_weight, adapter_down_weight, adapter_up_weight, tenant_row_counts, handoff_counts, tenant_gradient_slot):
    groups = handoff_counts.shape[0]
    capacity = input_rows.shape[0] // groups
    balanced_rows = cotangent.shape[0] // groups
    tenant_labels = adapter_up_weight.shape[0]
    source, source_row = balanced_sources(handoff_counts, balanced_rows)
    tenant_end = jnp.cumsum(tenant_row_counts, axis=1).astype(jnp.int32)
    row_tenant = jnp.sum((jnp.take(tenant_end, source, axis=0) <= source_row[:, None]).astype(jnp.int32), axis=1).astype(jnp.int32)
    home_index = (source * capacity + source_row).astype(jnp.int32)
    collected_rows = jnp.take(input_rows, home_index, axis=0)
    tenant_onehot = (row_tenant[:, None] == jnp.arange(tenant_labels, dtype=jnp.int32)[None, :]).astype(jnp.float32)
    lowered_gathered = jnp.einsum("ai,wiv->awv", collected_rows.astype(jnp.float32), adapter_down_weight.astype(jnp.float32))
    backward_gathered = jnp.einsum("ku,wxu->kwx", cotangent.astype(jnp.float32), adapter_up_weight.astype(jnp.float32))
    adapter_input = jnp.sum(lowered_gathered * tenant_onehot[:, :, None], axis=1).astype(jnp.bfloat16)
    adapter_gradient = (adapter_scale * jnp.sum(backward_gathered * tenant_onehot[:, :, None], axis=1)).astype(jnp.bfloat16)
    scattered_input = tenant_onehot[:, :, None] * adapter_input.astype(jnp.float32)[:, None, :]
    scattered_gradient = tenant_onehot[:, :, None] * adapter_gradient.astype(jnp.float32)[:, None, :]
    frozen_output = jnp.dot(collected_rows, frozen_weight, preferred_element_type=jnp.float32)
    adapter_output = jnp.einsum("hno,noa->ha", scattered_input, adapter_up_weight.astype(jnp.float32))
    outputs = (frozen_output + adapter_scale * adapter_output).astype(jnp.bfloat16)
    frozen_gradient = lax.dot_general(cotangent, frozen_weight, (((1,), (1,)), ((), ())), preferred_element_type=jnp.float32)
    adapter_backward = jnp.einsum("zwd,wid->zi", scattered_gradient, adapter_down_weight.astype(jnp.float32))
    balanced_input = (frozen_gradient + adapter_backward).astype(jnp.bfloat16)
    row_grad = jnp.zeros(input_rows.shape, jnp.bfloat16).at[home_index].set(balanced_input)
    summed_down = jnp.zeros(adapter_down_weight.shape, jnp.float32)
    summed_up = jnp.zeros(adapter_up_weight.shape, jnp.float32)
    for group in range(groups):
        leading_rows = group * balanced_rows
        rows_here = collected_rows[leading_rows:leading_rows + balanced_rows].astype(jnp.float32)
        part_a = jnp.einsum("mf,mtr->tfr", rows_here, scattered_gradient[leading_rows:leading_rows + balanced_rows])
        partial_up = adapter_scale * jnp.einsum("vkh,vz->khz", scattered_input[leading_rows:leading_rows + balanced_rows], cotangent[leading_rows:leading_rows + balanced_rows].astype(jnp.float32))
        round_a = lax.optimization_barrier(part_a.astype(jnp.bfloat16))
        round_b = lax.optimization_barrier(partial_up.astype(jnp.bfloat16))
        summed_down = summed_down + round_a.astype(jnp.float32)
        summed_up = summed_up + round_b.astype(jnp.float32)
    order = jnp.argsort(tenant_gradient_slot).astype(jnp.int32)
    grad_a = jnp.take(summed_down, order, axis=0).astype(jnp.bfloat16)
    grad_b = jnp.take(summed_up, order, axis=0).astype(jnp.bfloat16)
    return (outputs, row_grad, grad_a, grad_b)
```

```python
import functools

import jax
import jax.numpy as jnp
from jax import lax
from jax.experimental import pallas as pl
from jax.experimental.pallas import tpu as pltpu
from jax.sharding import PartitionSpec as P

adapter_scale = 0.25
BF = jnp.bfloat16
F32 = jnp.float32
I32 = jnp.int32
VMEM_LIMIT = 48 * 2**20


def before_sums(values, group_axis):
    return jnp.cumsum(values, axis=group_axis) - values


def find_source(starts, counts, length):
    places = jnp.arange(length, dtype=jnp.int32)[:, None]
    inside = (places >= starts[None, :]) & (places < (starts + counts)[None, :])
    numbers = jnp.arange(starts.shape[0], dtype=jnp.int32)[None, :]
    source = jnp.sum(jnp.where(inside, numbers, 0), axis=1)
    offset = places[:, 0] - jnp.sum(jnp.where(inside, starts[None, :], 0), axis=1)
    present = jnp.any(inside, axis=1)
    return (source, offset, present)


def pack_slots(values, starts, counts, width, allowed):
    places = jnp.arange(width, dtype=jnp.int32)[None, :]
    picked = jnp.minimum(starts[:, None] + places, values.shape[0] - 1)
    valid = (places < counts[:, None]) & allowed[:, None]
    taken = jnp.take(values, picked.reshape(-1), axis=0).reshape(
        counts.shape[0], width, values.shape[1]
    )
    return jnp.where(valid[:, :, None], taken, jnp.zeros((), values.dtype))


def plain_body(
    input_rows,
    cotangent,
    frozen_weight,
    adapter_down_weight,
    adapter_up_weight,
    tenant_row_counts,
    handoff_counts,
    tenant_gradient_slot,
):
    groups = lax.axis_size("dp")
    mine = lax.axis_index("dp")
    balanced_rows = cotangent.shape[0]
    capacity = input_rows.shape[0]
    feature_width = input_rows.shape[1]
    column_index = cotangent.shape[1]
    tenant_labels = adapter_up_weight.shape[0]
    group_position = adapter_up_weight.shape[1]
    sent_before = before_sums(handoff_counts, 1)
    recv_before = before_sums(handoff_counts, 0)
    my_sends = handoff_counts[mine]
    my_send_starts = sent_before[mine]
    my_recvs = handoff_counts[:, mine]
    my_recv_starts = recv_before[:, mine]
    others = jnp.arange(groups, dtype=jnp.int32) != mine
    source, offset, present = find_source(my_recv_starts, my_recvs, balanced_rows)
    source_row = sent_before[source, mine] + offset
    tenant_end = jnp.cumsum(tenant_row_counts, axis=1)
    row_tenant = jnp.sum(
        (jnp.take(tenant_end, source, axis=0) <= source_row[:, None]).astype(jnp.int32), axis=1
    )
    tenant_onehot = (
        row_tenant[:, None] == jnp.arange(tenant_labels, dtype=jnp.int32)[None, :]
    ).astype(jnp.bfloat16)
    half_slot = balanced_rows // 2
    outgoing = pack_slots(input_rows, my_send_starts, my_sends, half_slot, others)
    arrived = lax.all_to_all(outgoing, "dp", split_axis=0, concat_axis=0, tiled=True)
    pool = jnp.concatenate([arrived.reshape(groups * half_slot, feature_width), input_rows], axis=0)
    picked = jnp.where(source == mine, groups * half_slot + source_row, source * half_slot + offset)
    group_rows = jnp.take(pool, jnp.minimum(picked, pool.shape[0] - 1), axis=0)
    frozen_output = jnp.dot(
        lax.all_gather(group_rows, "fsdp", axis=1, tiled=True),
        frozen_weight,
        preferred_element_type=jnp.float32,
    )
    lowered_gathered = jnp.einsum(
        "ai,wiv->awv", group_rows, adapter_down_weight, preferred_element_type=jnp.float32
    )
    backward_gathered = jnp.einsum(
        "ku,wxu->kwx", cotangent, adapter_up_weight, preferred_element_type=jnp.float32
    )
    hot_wide = tenant_onehot.astype(jnp.float32)[:, :, None]
    down_part = jnp.sum(lowered_gathered * hot_wide, axis=1)
    back_part = jnp.sum(backward_gathered * hot_wide, axis=1)
    lowered_total, backward_total = lax.psum((down_part, back_part), "fsdp")
    adapter_input = lowered_total.astype(jnp.bfloat16)
    adapter_gradient = (adapter_scale * backward_total).astype(jnp.bfloat16)
    scattered_input = (tenant_onehot[:, :, None] * adapter_input[:, None, :]).reshape(
        balanced_rows, tenant_labels * group_position
    )
    scattered_gradient = (tenant_onehot[:, :, None] * adapter_gradient[:, None, :]).reshape(
        balanced_rows, tenant_labels * group_position
    )
    adapter_output = jnp.dot(
        scattered_input,
        adapter_up_weight.reshape(tenant_labels * group_position, column_index),
        preferred_element_type=jnp.float32,
    )
    adapter_backward = lax.dot_general(
        scattered_gradient,
        adapter_down_weight.transpose(1, 0, 2).reshape(
            feature_width, tenant_labels * group_position
        ),
        (((1,), (1,)), ((), ())),
        preferred_element_type=jnp.float32,
    )
    outputs = (frozen_output + adapter_scale * adapter_output).astype(jnp.bfloat16)
    grad_terms = lax.dot_general(
        cotangent, frozen_weight, (((1,), (1,)), ((), ())), preferred_element_type=jnp.float32
    )
    frozen_gradient = lax.psum_scatter(grad_terms, "fsdp", scatter_dimension=1, tiled=True)
    group_gradient = (frozen_gradient + adapter_backward).astype(jnp.bfloat16)
    part_a = lax.dot_general(
        group_rows, scattered_gradient, (((0,), (0,)), ((), ())), preferred_element_type=jnp.float32
    )
    part_a = part_a.reshape(feature_width, tenant_labels, group_position).transpose(1, 0, 2)
    partial_up = adapter_scale * lax.dot_general(
        scattered_input, cotangent, (((0,), (0,)), ((), ())), preferred_element_type=jnp.float32
    )
    partial_up = partial_up.reshape(tenant_labels, group_position, column_index)
    order = jnp.argsort(tenant_gradient_slot)
    share = tenant_labels // groups
    owner_a = (
        jnp.take(part_a, order, axis=0)
        .astype(jnp.bfloat16)
        .reshape(groups, share, feature_width, group_position)
    )
    owner_b = (
        jnp.take(partial_up, order, axis=0)
        .astype(jnp.bfloat16)
        .reshape(groups, share, group_position, column_index)
    )
    source_home, offset_home, present_home = find_source(my_send_starts, my_sends, capacity)
    half_slot = balanced_rows // 2
    back_slots = pack_slots(group_gradient, my_recv_starts, my_recvs, half_slot, others)
    home, sums_a, sums_b = (
        lax.all_to_all(back_slots, "dp", split_axis=0, concat_axis=0, tiled=True),
        lax.all_to_all(owner_a, "dp", split_axis=0, concat_axis=0, tiled=True),
        lax.all_to_all(owner_b, "dp", split_axis=0, concat_axis=0, tiled=True),
    )
    pool_home = jnp.concatenate(
        [home.reshape(groups * half_slot, feature_width), group_gradient], axis=0
    )
    picked_home = jnp.where(
        source_home == mine,
        groups * half_slot + recv_before[mine, mine] + offset_home,
        source_home * half_slot + offset_home,
    )
    row_grad = jnp.take(pool_home, jnp.minimum(picked_home, pool_home.shape[0] - 1), axis=0)
    row_grad = jnp.where(present_home[:, None], row_grad, jnp.zeros((), jnp.bfloat16))
    grad_a = jnp.sum(sums_a.astype(jnp.float32), axis=0).astype(jnp.bfloat16)
    grad_b = jnp.sum(sums_b.astype(jnp.float32), axis=0).astype(jnp.bfloat16)
    return (outputs, row_grad, grad_a, grad_b)


def params():
    return pltpu.CompilerParams(vmem_limit_bytes=VMEM_LIMIT)


def cost(flops, moved):
    return pl.CostEstimate(flops=int(flops), bytes_accessed=int(moved), transcendentals=0)


SMEM = functools.partial(pl.BlockSpec, memory_space=pltpu.SMEM)


def whole(shape):
    return pl.BlockSpec(shape, lambda *_: (0,) * len(shape))


def before(handoff_ref, giver, taker, groups):
    sent = jnp.int32(0)
    got = jnp.int32(0)
    for other in range(groups):
        sent = sent + jnp.where(other < taker, handoff_ref[giver, other], 0)
        got = got + jnp.where(other < giver, handoff_ref[other, taker], 0)
    return sent, got


def pack(place, handoff, counts, slots, rows, balanced, half):
    groups, tenants = counts.shape
    capacity, width = rows.shape

    def kernel(place_ref, handoff_ref, slots_ref, counts_ref, rows_ref, *outs):
        out_refs, tenant_ref, slot_ref = outs[: groups - 1], outs[groups - 1], outs[groups]
        mine = place_ref[0]
        here = lax.broadcasted_iota(I32, (half, capacity), 1)
        slot = lax.broadcasted_iota(I32, (half, capacity), 0)
        for step in range(1, groups):
            partner = mine ^ step
            sent, _ = before(handoff_ref, mine, partner, groups)
            pick = (here == slot + sent) & (slot < handoff_ref[mine, partner])
            out_refs[step - 1][...] = jnp.dot(
                pick.astype(F32).astype(BF), rows_ref[...], preferred_element_type=F32
            ).astype(BF)
        upto = lax.broadcasted_iota(I32, (tenants, tenants), 1) <= lax.broadcasted_iota(
            I32, (tenants, tenants), 0
        )
        ends = lax.dot_general(
            upto.astype(F32).astype(BF),
            counts_ref[...].astype(F32).astype(BF),
            (((1,), (1,)), ((), ())),
            preferred_element_type=F32,
        ).astype(I32)
        place_of = lax.broadcasted_iota(I32, (1, balanced), 1)
        for step in range(groups):
            taker = mine ^ step
            position = place_of
            row_ends = jnp.zeros((tenants, balanced), I32)
            for giver in range(groups):
                sent, got = before(handoff_ref, giver, taker, groups)
                inside = (place_of >= got) & (place_of < got + handoff_ref[giver, taker])
                position = position + jnp.where(inside, sent - got, 0)
                row_ends = row_ends + jnp.where(inside, ends[:, giver : giver + 1], 0)
            tenant = jnp.sum((row_ends <= position).astype(I32), axis=0, keepdims=True)
            target = jnp.zeros((1, balanced), I32)
            for label in range(tenants):
                target = target + jnp.where(tenant == label, slots_ref[label], 0)
            tenant_ref[step : step + 1, :] = tenant
            slot_ref[step : step + 1, :] = target

    return pl.pallas_call(
        kernel,
        in_specs=[SMEM(), SMEM(), SMEM(), pl.BlockSpec(memory_space=pltpu.VMEM), pl.BlockSpec(memory_space=pltpu.VMEM)],
        out_shape=[jax.ShapeDtypeStruct((half, width), BF)] * (groups - 1)
        + [jax.ShapeDtypeStruct((groups, balanced), I32)] * 2,
        compiler_params=params(),
        cost_estimate=cost(2 * 3 * half * capacity * width, 2 * capacity * width * 2),
    )(place, handoff, slots, counts, rows)


def masked_rank(product, tenant, first, rank):
    total = jnp.zeros((rank, product.shape[1]), F32)
    for label in range(product.shape[0] // rank):
        total = total + jnp.where(tenant == first + label, product[label * rank : (label + 1) * rank], 0.0)
    return total


def unpack(place, handoff, tenant, rows, arrived, down, rank, block):
    groups, balanced = tenant.shape
    capacity, width = rows.shape
    half = arrived[0].shape[0]

    def kernel(place_ref, handoff_ref, tenant_ref, rows_ref, *refs):
        arrived_refs = refs[: groups - 1]
        down_ref, gathered_ref, lowered_ref, turned = refs[groups - 1 :]
        step = pl.program_id(0)

        @pl.when(step == 0)
        def _():
            mine = place_ref[0]
            place_of = lax.broadcasted_iota(I32, (balanced, capacity), 0)
            here = lax.broadcasted_iota(I32, (balanced, capacity), 1)
            sent, got = before(handoff_ref, mine, mine, groups)
            inside = (place_of >= got) & (place_of < got + handoff_ref[mine, mine])
            pick = inside & (here == place_of - got + sent)
            total = jnp.dot(pick.astype(F32).astype(BF), rows_ref[...], preferred_element_type=F32)
            place_of = lax.broadcasted_iota(I32, (balanced, half), 0)
            here = lax.broadcasted_iota(I32, (balanced, half), 1)
            for k in range(1, groups):
                giver = mine ^ k
                _, got = before(handoff_ref, giver, mine, groups)
                inside = (place_of >= got) & (place_of < got + handoff_ref[giver, mine])
                pick = inside & (here == place_of - got)
                total = total + jnp.dot(
                    pick.astype(F32).astype(BF), arrived_refs[k - 1][...], preferred_element_type=F32
                )
            gathered_ref[...] = total.astype(BF)
            turned[...] = total.T.astype(BF)
            lowered_ref[...] = jnp.zeros_like(lowered_ref)

        product = jnp.dot(down_ref[...], turned[...], preferred_element_type=F32)
        lowered_ref[...] += masked_rank(product, tenant_ref[0:1, :], step * (block // rank), rank)

    return pl.pallas_call(
        kernel,
        grid=(down.shape[0] // block,),
        in_specs=[SMEM(), SMEM(), whole((groups, balanced)), whole((capacity, width))]
        + [whole((half, width))] * (groups - 1)
        + [pl.BlockSpec((block, width), lambda i: (i, 0))],
        out_specs=[whole((balanced, width)), whole((rank, balanced))],
        out_shape=[
            jax.ShapeDtypeStruct((balanced, width), BF),
            jax.ShapeDtypeStruct((rank, balanced), F32),
        ],
        scratch_shapes=[pltpu.VMEM((width, balanced), BF)],
        compiler_params=params(),
        cost_estimate=cost(2 * balanced * down.size, 2 * down.size + 6 * balanced * width),
    )(place, handoff, tenant, rows, *arrived, down)


def rank_backward(tenant, turned, up, rank, block):
    balanced = turned.shape[1]
    hidden = up.shape[1]

    def kernel(tenant_ref, turned_ref, up_ref, out_ref):
        step = pl.program_id(0)
        product = jnp.dot(up_ref[...], turned_ref[...], preferred_element_type=F32)
        mine = masked_rank(product, tenant_ref[0:1, :], step * (block // rank), rank)

        @pl.when(step == 0)
        def _():
            out_ref[...] = mine

        @pl.when(step > 0)
        def _():
            out_ref[...] += mine

    return pl.pallas_call(
        kernel,
        grid=(up.shape[0] // block,),
        in_specs=[whole(tenant.shape), whole(turned.shape), pl.BlockSpec((block, hidden), lambda i: (i, 0))],
        out_specs=whole((rank, balanced)),
        out_shape=jax.ShapeDtypeStruct((rank, balanced), F32),
        compiler_params=params(),
        cost_estimate=cost(2 * balanced * up.size, 2 * up.size),
    )(tenant, turned, up)


def base_gradient(owner, turned, weight, width, block, arrived=None):
    hidden, balanced = turned.shape
    steps = width // block

    def kernel(owner_ref, turned_ref, weight_ref, *refs):
        product = jnp.dot(weight_ref[...], turned_ref[...], preferred_element_type=F32).T
        if arrived is not None:
            product = product + refs[0][...].astype(F32)
        refs[-1][...] = product.astype(BF)

    piece = pl.BlockSpec((balanced, block), lambda i, owner_ref: (0, i))
    return pl.pallas_call(
        kernel,
        grid_spec=pltpu.PrefetchScalarGridSpec(
            num_scalar_prefetch=1,
            grid=(steps,),
            in_specs=[
                whole(turned.shape),
                pl.BlockSpec((block, hidden), lambda i, owner_ref: (owner_ref[0] * steps + i, 0)),
            ]
            + ([] if arrived is None else [piece]),
            out_specs=piece,
        ),
        out_shape=jax.ShapeDtypeStruct((balanced, width), BF),
        compiler_params=params(),
        cost_estimate=cost(2 * balanced * width * hidden, 2 * width * hidden),
    )(owner, turned, weight, *(() if arrived is None else (arrived,)))


def spread(wide_ref, column_ref, twice_ref, tenants, rank):
    lanes = 2 * rank
    odd = (lax.broadcasted_iota(I32, (column_ref.shape[0], lanes), 1) >= rank).astype(I32)
    label = column_ref[...] - odd
    for pair in range(tenants // 2):
        wide_ref[:, pair * lanes : (pair + 1) * lanes] = jnp.where(
            label == 2 * pair, twice_ref[...].astype(F32), 0.0
        ).astype(BF)


def forward(owners, parts, weight, block, total=None, column=None, twice=None, up=None, rank=None):
    balanced, width = parts[0].shape
    hidden = weight.shape[1]
    count = len(parts)
    last = up is not None

    def kernel(owners_ref, *refs):
        part_refs, weight_refs = refs[:count], refs[count : 2 * count]
        rest = list(refs[2 * count :])
        value = jnp.dot(part_refs[0][...], weight_refs[0][...], preferred_element_type=F32)
        for i in range(1, count):
            value = value + jnp.dot(part_refs[i][...], weight_refs[i][...], preferred_element_type=F32)
        if total is not None:
            value = value + rest.pop(0)[...]
        if last:
            column_ref, twice_ref, up_ref = rest.pop(0), rest.pop(0), rest.pop(0)
            wide_ref = rest.pop()

            @pl.when(pl.program_id(0) == 0)
            def _():
                spread(wide_ref, column_ref, twice_ref, up.shape[0] // rank, rank)

            value = value + jnp.dot(wide_ref[...], up_ref[...], preferred_element_type=F32)
        rest[0][...] = value.astype(rest[0].dtype)

    piece = pl.BlockSpec((balanced, block), lambda i, o: (0, i))
    in_specs = [whole((balanced, width))] * count
    for i in range(count):
        in_specs.append(pl.BlockSpec((width, block), lambda n, o, i=i: (o[i], n)))
    operands = [*parts, *([weight] * count)]
    if total is not None:
        in_specs.append(piece)
        operands.append(total)
    if last:
        in_specs += [whole(column.shape), whole(twice.shape), pl.BlockSpec((up.shape[0], block), lambda i, o: (0, i))]
        operands += [column, twice, up]
    return pl.pallas_call(
        kernel,
        grid_spec=pltpu.PrefetchScalarGridSpec(
            num_scalar_prefetch=1,
            grid=(hidden // block,),
            in_specs=in_specs,
            out_specs=piece,
            scratch_shapes=[pltpu.VMEM((balanced, up.shape[0]), BF)] if last else [],
        ),
        out_shape=jax.ShapeDtypeStruct((balanced, hidden), BF if last else F32),
        compiler_params=params(),
        cost_estimate=cost(
            2 * balanced * hidden * (count * width + (up.shape[0] if last else 0)),
            2 * hidden * (count * width + (up.shape[0] if last else 0)),
        ),
    )(owners, *operands)


def finish_gradient(terms, column, twice, down, block, rank):
    balanced, width = terms[0].shape

    def kernel(column_ref, twice_ref, down_ref, *refs):
        term_refs, out_ref, wide_ref = refs[:-2], refs[-2], refs[-1]

        @pl.when(pl.program_id(0) == 0)
        def _():
            spread(wide_ref, column_ref, twice_ref, down.shape[0] // rank, rank)

        value = jnp.dot(wide_ref[...], down_ref[...], preferred_element_type=F32)
        for term_ref in term_refs:
            value = value + term_ref[...].astype(F32)
        out_ref[...] = value.astype(BF)

    piece = pl.BlockSpec((balanced, block), lambda i: (0, i))
    return pl.pallas_call(
        kernel,
        grid=(width // block,),
        in_specs=[whole(column.shape), whole(twice.shape), pl.BlockSpec((down.shape[0], block), lambda i: (0, i))]
        + [piece] * len(terms),
        out_specs=piece,
        out_shape=jax.ShapeDtypeStruct((balanced, width), BF),
        scratch_shapes=[pltpu.VMEM((balanced, down.shape[0]), BF)],
        compiler_params=params(),
        cost_estimate=cost(2 * balanced * down.size, 2 * down.size),
    )(column, twice, down, *terms)


def owned_gradient(place, slot, ranks, values, share, scale, block):
    groups, balanced = slot.shape
    rank = ranks[0].shape[0]
    width = values[0].shape[1]

    def kernel(place_ref, slot_ref, *refs):
        rank_refs, value_refs = refs[:groups], refs[groups : 2 * groups]
        out_ref, wide_ref = refs[2 * groups :]

        @pl.when(pl.program_id(0) == 0)
        def _():
            first = place_ref[0] * share
            for k in range(groups):
                for s in range(share):
                    wide_ref[k, s * rank : (s + 1) * rank, :] = jnp.where(
                        slot_ref[k : k + 1, :] == first + s, rank_refs[k][...].astype(F32), 0.0
                    ).astype(BF)

        value = jnp.dot(wide_ref[0], value_refs[0][...], preferred_element_type=F32)
        for k in range(1, groups):
            value = value + jnp.dot(wide_ref[k], value_refs[k][...], preferred_element_type=F32)
        out_ref[...] = (scale * value).astype(BF)

    return pl.pallas_call(
        kernel,
        grid=(width // block,),
        in_specs=[SMEM(), whole(slot.shape)]
        + [whole((rank, balanced))] * groups
        + [pl.BlockSpec((balanced, block), lambda i: (0, i))] * groups,
        out_specs=pl.BlockSpec((share * rank, block), lambda i: (0, i)),
        out_shape=jax.ShapeDtypeStruct((share * rank, width), BF),
        scratch_shapes=[pltpu.VMEM((groups, share * rank, balanced), BF)],
        compiler_params=params(),
        cost_estimate=cost(2 * groups * balanced * share * rank * width, 2 * width * (groups * balanced + share * rank)),
    )(place, slot, *ranks, *values)


def bring_home(place, handoff, gradients, capacity):
    balanced, width = gradients[0].shape
    groups = handoff.shape[0]

    def kernel(place_ref, handoff_ref, *refs):
        out_ref = refs[-1]
        mine = place_ref[0]
        row = lax.broadcasted_iota(I32, (capacity, balanced), 0)
        here = lax.broadcasted_iota(I32, (capacity, balanced), 1)
        total = jnp.zeros((capacity, width), F32)
        for k in range(groups):
            taker = mine ^ k
            sent, got = before(handoff_ref, mine, taker, groups)
            inside = (row >= sent) & (row < sent + handoff_ref[mine, taker])
            pick = inside & (here == row - sent + got)
            total = total + jnp.dot(pick.astype(F32).astype(BF), refs[k][...], preferred_element_type=F32)
        out_ref[...] = total.astype(BF)

    return pl.pallas_call(
        kernel,
        in_specs=[SMEM(), SMEM()] + [pl.BlockSpec(memory_space=pltpu.VMEM)] * groups,
        out_shape=jax.ShapeDtypeStruct((capacity, width), BF),
        compiler_params=params(),
        cost_estimate=cost(2 * groups * balanced * capacity * width, 4 * groups * balanced * width),
    )(place, handoff, *gradients)


def swap(values, axis, distance):
    size = lax.axis_size(axis)
    return lax.ppermute(values, axis, [(i, i ^ distance) for i in range(size)])


def after(values, *earlier):
    return lax.optimization_barrier((values, *earlier))[0]


def fast_body(
    input_rows,
    cotangent,
    frozen_weight,
    adapter_down_weight,
    adapter_up_weight,
    tenant_row_counts,
    handoff_counts,
    tenant_gradient_slot,
):
    mine = lax.axis_index("dp")
    z = lax.axis_index("fsdp")
    balanced = cotangent.shape[0]
    capacity, width = input_rows.shape
    tenants, rank, hidden = adapter_up_weight.shape
    share = tenants // lax.axis_size("dp")
    place = mine.astype(I32).reshape(1)
    owner = [(z ^ k).astype(I32) for k in range(4)]
    down = adapter_down_weight.transpose(0, 2, 1).reshape(tenants * rank, width)
    up = adapter_up_weight.reshape(tenants * rank, hidden)
    turned = cotangent.T

    *outgoing, tenant, slot = pack(
        place, handoff_counts, tenant_row_counts, tenant_gradient_slot, input_rows, balanced, balanced // 2
    )
    arrived = [None] * 3
    for k in (2, 3, 1):
        arrived[k - 1] = swap(outgoing[k - 1], "dp", k)

    far = base_gradient(owner[3].reshape(1), turned, frozen_weight, width, 512)
    for_far = swap(far, "fsdp", 1)
    near = base_gradient(owner[1].reshape(1), turned, frozen_weight, width, 512)
    from_near = swap(near, "fsdp", 1)
    raised = rank_backward(tenant, turned, up, rank, 512)
    gathered, lowered = unpack(place, handoff_counts, tenant, input_rows, arrived, down, rank, 512)
    pair = swap(gathered, "fsdp", 2)
    beside = swap(gathered, "fsdp", 1)
    across = base_gradient(owner[2].reshape(1), turned, frozen_weight, width, 512, for_far)
    from_pair = swap(across, "fsdp", 2)
    cot_x = swap(after(cotangent, gathered), "dp", 2)
    diagonal = swap(pair, "fsdp", 1)

    partial = jnp.concatenate([lowered, raised], axis=0)
    summed = partial + swap(partial, "fsdp", 1)
    summed = summed + swap(partial, "fsdp", 2) + swap(partial, "fsdp", 3)
    lora_in = summed[:rank].astype(BF)
    lora_grad = (adapter_scale * summed[rank:]).astype(BF)
    ranks = jnp.concatenate([lora_in, lora_grad], axis=0)
    all_ranks = [ranks] + [swap(ranks, "dp", k) for k in (1, 2, 3)]
    column = tenant[0].reshape(balanced, 1)
    twice_in = jnp.concatenate([lora_in * jnp.asarray(adapter_scale, BF)] * 2, axis=0).T
    twice_grad = jnp.concatenate([lora_grad] * 2, axis=0).T

    own = base_gradient(owner[0].reshape(1), turned, frozen_weight, width, 512)
    total = forward(jnp.stack([owner[0], owner[1]]), [gathered, beside], frozen_weight, 512)
    group_gradient = finish_gradient([own, from_near, from_pair], column, twice_grad, down, 512, rank)

    gathered_x = swap(after(gathered, cot_x), "dp", 2)
    cot_all = [cotangent, swap(cotangent, "dp", 1), cot_x, swap(cot_x, "dp", 1)]
    gathered_all = [gathered, swap(gathered, "dp", 1), gathered_x, swap(gathered_x, "dp", 1)]
    back_x = swap(group_gradient, "dp", 2)
    back = [group_gradient, swap(group_gradient, "dp", 1), back_x, swap(back_x, "dp", 1)]

    outputs = forward(
        jnp.stack([owner[2], owner[3]]), [pair, diagonal], frozen_weight, 512,
        total, column, twice_in, up, rank,
    )
    grad_b = owned_gradient(
        place, slot, [r[:rank] for r in all_ranks], cot_all, share, adapter_scale, 1024
    )
    grad_a = owned_gradient(place, slot, [r[rank:] for r in all_ranks], gathered_all, share, 1.0, 512)
    row_grad = bring_home(place, handoff_counts, back, capacity)
    return (
        outputs,
        row_grad,
        grad_a.reshape(share, rank, width).transpose(0, 2, 1),
        grad_b.reshape(share, rank, hidden),
    )


def solution(mesh):
    placed = (
        P(("groups", "dp"), "fsdp"),
        P(("groups", "dp"), "fsdp"),
        P(None, "fsdp"),
        P("groups", "fsdp", None),
        P("groups", None, "fsdp"),
        P("groups", None),
        P("groups", None),
        P("groups"),
    )
    four_by_four = mesh.shape["dp"] == 4 and mesh.shape["fsdp"] == 4
    return jax.shard_map(
        fast_body if four_by_four else plain_body,
        mesh=mesh,
        in_specs=placed,
        out_specs=(
            P(("groups", "dp"), "fsdp"),
            P(("groups", "dp"), "fsdp"),
            P(("groups", "dp"), "fsdp", None),
            P(("groups", "dp"), None, "fsdp"),
        ),
        check_vma=False,
    )
```

```python
import functools

import jax
import jax.numpy as jnp
from jax import lax
from jax.experimental import pallas as pl
from jax.experimental.pallas import tpu as pltpu
from jax.sharding import PartitionSpec as P

adapter_scale = 0.25
BF = jnp.bfloat16
F32 = jnp.float32
I32 = jnp.int32
VMEM_LIMIT = 48 * 2**20


def before_sums(values, group_axis):
    return jnp.cumsum(values, axis=group_axis) - values


def find_source(starts, counts, length):
    places = jnp.arange(length, dtype=jnp.int32)[:, None]
    inside = (places >= starts[None, :]) & (places < (starts + counts)[None, :])
    numbers = jnp.arange(starts.shape[0], dtype=jnp.int32)[None, :]
    source = jnp.sum(jnp.where(inside, numbers, 0), axis=1)
    offset = places[:, 0] - jnp.sum(jnp.where(inside, starts[None, :], 0), axis=1)
    present = jnp.any(inside, axis=1)
    return (source, offset, present)


def pack_slots(values, starts, counts, width, allowed):
    places = jnp.arange(width, dtype=jnp.int32)[None, :]
    picked = jnp.minimum(starts[:, None] + places, values.shape[0] - 1)
    valid = (places < counts[:, None]) & allowed[:, None]
    taken = jnp.take(values, picked.reshape(-1), axis=0).reshape(
        counts.shape[0], width, values.shape[1]
    )
    return jnp.where(valid[:, :, None], taken, jnp.zeros((), values.dtype))


def plain_body(
    input_rows,
    cotangent,
    frozen_weight,
    adapter_down_weight,
    adapter_up_weight,
    tenant_row_counts,
    handoff_counts,
    tenant_gradient_slot,
):
    groups = lax.axis_size("dp")
    mine = lax.axis_index("dp")
    balanced_rows = cotangent.shape[0]
    capacity = input_rows.shape[0]
    feature_width = input_rows.shape[1]
    column_index = cotangent.shape[1]
    tenant_labels = adapter_up_weight.shape[0]
    group_position = adapter_up_weight.shape[1]
    sent_before = before_sums(handoff_counts, 1)
    recv_before = before_sums(handoff_counts, 0)
    my_sends = handoff_counts[mine]
    my_send_starts = sent_before[mine]
    my_recvs = handoff_counts[:, mine]
    my_recv_starts = recv_before[:, mine]
    others = jnp.arange(groups, dtype=jnp.int32) != mine
    source, offset, present = find_source(my_recv_starts, my_recvs, balanced_rows)
    source_row = sent_before[source, mine] + offset
    tenant_end = jnp.cumsum(tenant_row_counts, axis=1)
    row_tenant = jnp.sum(
        (jnp.take(tenant_end, source, axis=0) <= source_row[:, None]).astype(jnp.int32), axis=1
    )
    tenant_onehot = (
        row_tenant[:, None] == jnp.arange(tenant_labels, dtype=jnp.int32)[None, :]
    ).astype(jnp.bfloat16)
    half_slot = balanced_rows // 2
    outgoing = pack_slots(input_rows, my_send_starts, my_sends, half_slot, others)
    arrived = lax.all_to_all(outgoing, "dp", split_axis=0, concat_axis=0, tiled=True)
    pool = jnp.concatenate([arrived.reshape(groups * half_slot, feature_width), input_rows], axis=0)
    picked = jnp.where(source == mine, groups * half_slot + source_row, source * half_slot + offset)
    group_rows = jnp.take(pool, jnp.minimum(picked, pool.shape[0] - 1), axis=0)
    frozen_output = jnp.dot(
        lax.all_gather(group_rows, "fsdp", axis=1, tiled=True),
        frozen_weight,
        preferred_element_type=jnp.float32,
    )
    lowered_gathered = jnp.einsum(
        "ai,wiv->awv", group_rows, adapter_down_weight, preferred_element_type=jnp.float32
    )
    backward_gathered = jnp.einsum(
        "ku,wxu->kwx", cotangent, adapter_up_weight, preferred_element_type=jnp.float32
    )
    hot_wide = tenant_onehot.astype(jnp.float32)[:, :, None]
    down_part = jnp.sum(lowered_gathered * hot_wide, axis=1)
    back_part = jnp.sum(backward_gathered * hot_wide, axis=1)
    lowered_total, backward_total = lax.psum((down_part, back_part), "fsdp")
    adapter_input = lowered_total.astype(jnp.bfloat16)
    adapter_gradient = (adapter_scale * backward_total).astype(jnp.bfloat16)
    scattered_input = (tenant_onehot[:, :, None] * adapter_input[:, None, :]).reshape(
        balanced_rows, tenant_labels * group_position
    )
    scattered_gradient = (tenant_onehot[:, :, None] * adapter_gradient[:, None, :]).reshape(
        balanced_rows, tenant_labels * group_position
    )
    adapter_output = jnp.dot(
        scattered_input,
        adapter_up_weight.reshape(tenant_labels * group_position, column_index),
        preferred_element_type=jnp.float32,
    )
    adapter_backward = lax.dot_general(
        scattered_gradient,
        adapter_down_weight.transpose(1, 0, 2).reshape(
            feature_width, tenant_labels * group_position
        ),
        (((1,), (1,)), ((), ())),
        preferred_element_type=jnp.float32,
    )
    outputs = (frozen_output + adapter_scale * adapter_output).astype(jnp.bfloat16)
    grad_terms = lax.dot_general(
        cotangent, frozen_weight, (((1,), (1,)), ((), ())), preferred_element_type=jnp.float32
    )
    frozen_gradient = lax.psum_scatter(grad_terms, "fsdp", scatter_dimension=1, tiled=True)
    group_gradient = (frozen_gradient + adapter_backward).astype(jnp.bfloat16)
    part_a = lax.dot_general(
        group_rows, scattered_gradient, (((0,), (0,)), ((), ())), preferred_element_type=jnp.float32
    )
    part_a = part_a.reshape(feature_width, tenant_labels, group_position).transpose(1, 0, 2)
    partial_up = adapter_scale * lax.dot_general(
        scattered_input, cotangent, (((0,), (0,)), ((), ())), preferred_element_type=jnp.float32
    )
    partial_up = partial_up.reshape(tenant_labels, group_position, column_index)
    order = jnp.argsort(tenant_gradient_slot)
    share = tenant_labels // groups
    owner_a = (
        jnp.take(part_a, order, axis=0)
        .astype(jnp.bfloat16)
        .reshape(groups, share, feature_width, group_position)
    )
    owner_b = (
        jnp.take(partial_up, order, axis=0)
        .astype(jnp.bfloat16)
        .reshape(groups, share, group_position, column_index)
    )
    source_home, offset_home, present_home = find_source(my_send_starts, my_sends, capacity)
    half_slot = balanced_rows // 2
    back_slots = pack_slots(group_gradient, my_recv_starts, my_recvs, half_slot, others)
    home, sums_a, sums_b = (
        lax.all_to_all(back_slots, "dp", split_axis=0, concat_axis=0, tiled=True),
        lax.all_to_all(owner_a, "dp", split_axis=0, concat_axis=0, tiled=True),
        lax.all_to_all(owner_b, "dp", split_axis=0, concat_axis=0, tiled=True),
    )
    pool_home = jnp.concatenate(
        [home.reshape(groups * half_slot, feature_width), group_gradient], axis=0
    )
    picked_home = jnp.where(
        source_home == mine,
        groups * half_slot + recv_before[mine, mine] + offset_home,
        source_home * half_slot + offset_home,
    )
    row_grad = jnp.take(pool_home, jnp.minimum(picked_home, pool_home.shape[0] - 1), axis=0)
    row_grad = jnp.where(present_home[:, None], row_grad, jnp.zeros((), jnp.bfloat16))
    grad_a = jnp.sum(sums_a.astype(jnp.float32), axis=0).astype(jnp.bfloat16)
    grad_b = jnp.sum(sums_b.astype(jnp.float32), axis=0).astype(jnp.bfloat16)
    return (outputs, row_grad, grad_a, grad_b)


def params(limit=VMEM_LIMIT):
    return pltpu.CompilerParams(vmem_limit_bytes=limit)


def cost(flops, moved):
    return pl.CostEstimate(flops=int(flops) // 1000, bytes_accessed=int(moved) // 1000, transcendentals=0)


SMEM = functools.partial(pl.BlockSpec, memory_space=pltpu.SMEM)


def whole(shape):
    return pl.BlockSpec(shape, lambda *_: (0,) * len(shape))


def before(handoff_ref, giver, taker, groups):
    sent = jnp.int32(0)
    got = jnp.int32(0)
    for other in range(groups):
        sent = sent + jnp.where(other < taker, handoff_ref[giver, other], 0)
        got = got + jnp.where(other < giver, handoff_ref[other, taker], 0)
    return sent, got


def pack(place, handoff, counts, slots, rows, balanced, half):
    groups, tenants = counts.shape
    capacity, width = rows.shape

    def kernel(place_ref, handoff_ref, slots_ref, counts_ref, rows_ref, *outs):
        out_refs, tenant_ref, slot_ref = outs[: groups - 1], outs[groups - 1], outs[groups]
        mine = place_ref[0]
        here = lax.broadcasted_iota(I32, (half, capacity), 1)
        slot = lax.broadcasted_iota(I32, (half, capacity), 0)
        for step in range(1, groups):
            partner = mine ^ step
            sent, _ = before(handoff_ref, mine, partner, groups)
            pick = (here == slot + sent) & (slot < handoff_ref[mine, partner])
            out_refs[step - 1][...] = jnp.dot(
                pick.astype(F32).astype(BF), rows_ref[...], preferred_element_type=F32
            ).astype(BF)
        upto = lax.broadcasted_iota(I32, (tenants, tenants), 1) <= lax.broadcasted_iota(
            I32, (tenants, tenants), 0
        )
        ends = lax.dot_general(
            upto.astype(F32).astype(BF),
            counts_ref[...].astype(F32).astype(BF),
            (((1,), (1,)), ((), ())),
            preferred_element_type=F32,
        ).astype(I32)
        place_of = lax.broadcasted_iota(I32, (1, balanced), 1)
        for step in range(groups):
            taker = mine ^ step
            position = place_of
            row_ends = jnp.zeros((tenants, balanced), I32)
            for giver in range(groups):
                sent, got = before(handoff_ref, giver, taker, groups)
                inside = (place_of >= got) & (place_of < got + handoff_ref[giver, taker])
                position = position + jnp.where(inside, sent - got, 0)
                row_ends = row_ends + jnp.where(inside, ends[:, giver : giver + 1], 0)
            tenant = jnp.sum((row_ends <= position).astype(I32), axis=0, keepdims=True)
            target = jnp.zeros((1, balanced), I32)
            for label in range(tenants):
                target = target + jnp.where(tenant == label, slots_ref[label], 0)
            tenant_ref[step : step + 1, :] = tenant
            slot_ref[step : step + 1, :] = target

    return pl.pallas_call(
        kernel,
        in_specs=[SMEM(), SMEM(), SMEM(), pl.BlockSpec(memory_space=pltpu.VMEM), pl.BlockSpec(memory_space=pltpu.VMEM)],
        out_shape=[jax.ShapeDtypeStruct((half, width), BF)] * (groups - 1)
        + [jax.ShapeDtypeStruct((groups, balanced), I32)] * 2,
        compiler_params=params(60 * 2**20),
        cost_estimate=cost(2 * 3 * half * capacity * width, 2 * capacity * width * 2),
    )(place, handoff, slots, counts, rows)


def masked_rank(product, tenant, first, rank):
    total = jnp.zeros((rank, product.shape[1]), F32)
    for label in range(product.shape[0] // rank):
        total = total + jnp.where(tenant == first + label, product[label * rank : (label + 1) * rank], 0.0)
    return total


def unpack(place, handoff, tenant, rows, arrived, down, rank, block):
    groups, balanced = tenant.shape
    capacity, width = rows.shape
    half = arrived[0].shape[0]

    def kernel(place_ref, handoff_ref, tenant_ref, rows_ref, *refs):
        arrived_refs = refs[: groups - 1]
        down_ref, gathered_ref, lowered_ref, turned = refs[groups - 1 :]
        step = pl.program_id(0)

        @pl.when(step == 0)
        def _():
            mine = place_ref[0]
            place_of = lax.broadcasted_iota(I32, (balanced, capacity), 0)
            here = lax.broadcasted_iota(I32, (balanced, capacity), 1)
            sent, got = before(handoff_ref, mine, mine, groups)
            inside = (place_of >= got) & (place_of < got + handoff_ref[mine, mine])
            pick = inside & (here == place_of - got + sent)
            total = jnp.dot(pick.astype(F32).astype(BF), rows_ref[...], preferred_element_type=F32)
            place_of = lax.broadcasted_iota(I32, (balanced, half), 0)
            here = lax.broadcasted_iota(I32, (balanced, half), 1)
            for k in range(1, groups):
                giver = mine ^ k
                _, got = before(handoff_ref, giver, mine, groups)
                inside = (place_of >= got) & (place_of < got + handoff_ref[giver, mine])
                pick = inside & (here == place_of - got)
                total = total + jnp.dot(
                    pick.astype(F32).astype(BF), arrived_refs[k - 1][...], preferred_element_type=F32
                )
            gathered_ref[...] = total.astype(BF)
            turned[...] = total.T.astype(BF)
            lowered_ref[...] = jnp.zeros_like(lowered_ref)

        product = jnp.dot(down_ref[...], turned[...], preferred_element_type=F32)
        lowered_ref[...] += masked_rank(product, tenant_ref[0:1, :], step * (block // rank), rank)

    return pl.pallas_call(
        kernel,
        grid=(down.shape[0] // block,),
        in_specs=[SMEM(), SMEM(), whole((groups, balanced)), whole((capacity, width))]
        + [whole((half, width))] * (groups - 1)
        + [pl.BlockSpec((block, width), lambda i: (i, 0))],
        out_specs=[whole((balanced, width)), whole((rank, balanced))],
        out_shape=[
            jax.ShapeDtypeStruct((balanced, width), BF),
            jax.ShapeDtypeStruct((rank, balanced), F32),
        ],
        scratch_shapes=[pltpu.VMEM((width, balanced), BF)],
        compiler_params=params(),
        cost_estimate=cost(2 * balanced * down.size, 2 * down.size + 6 * balanced * width),
    )(place, handoff, tenant, rows, *arrived, down)


def rank_backward(tenant, turned, up, lowered, block):
    rank, balanced = lowered.shape
    hidden = up.shape[1]
    steps = up.shape[0] // block

    def kernel(tenant_ref, turned_ref, lowered_ref, up_ref, out_ref, total_ref):
        step = pl.program_id(0)

        @pl.when(step == 0)
        def _():
            total_ref[:rank, :] = lowered_ref[...]
            total_ref[rank:, :] = jnp.zeros((rank, balanced), F32)

        product = jnp.dot(up_ref[...], turned_ref[...], preferred_element_type=F32)
        total_ref[rank:, :] += masked_rank(product, tenant_ref[0:1, :], step * (block // rank), rank)

        @pl.when(step == steps - 1)
        def _():
            out_ref[...] = total_ref[...].T

    return pl.pallas_call(
        kernel,
        grid=(steps,),
        in_specs=[
            whole(tenant.shape), whole(turned.shape), whole(lowered.shape),
            pl.BlockSpec((block, hidden), lambda i: (i, 0)),
        ],
        out_specs=whole((balanced, 2 * rank)),
        out_shape=jax.ShapeDtypeStruct((balanced, 2 * rank), F32),
        scratch_shapes=[pltpu.VMEM((2 * rank, balanced), F32)],
        compiler_params=params(),
        cost_estimate=cost(2 * balanced * up.size, 2 * up.size),
    )(tenant, turned, lowered, up)


def base_gradient(owner, turned, weight, width, block, arrived=None):
    hidden, balanced = turned.shape
    steps = width // block

    def kernel(owner_ref, turned_ref, weight_ref, *refs):
        product = jnp.dot(weight_ref[...], turned_ref[...], preferred_element_type=F32).T
        if arrived is not None:
            product = product + refs[0][...].astype(F32)
        refs[-1][...] = product.astype(BF)

    piece = pl.BlockSpec((balanced, block), lambda i, owner_ref: (0, i))
    return pl.pallas_call(
        kernel,
        grid_spec=pltpu.PrefetchScalarGridSpec(
            num_scalar_prefetch=1,
            grid=(steps,),
            in_specs=[
                whole(turned.shape),
                pl.BlockSpec((block, hidden), lambda i, owner_ref: (owner_ref[0] * steps + i, 0)),
            ]
            + ([] if arrived is None else [piece]),
            out_specs=piece,
        ),
        out_shape=jax.ShapeDtypeStruct((balanced, width), BF),
        compiler_params=params(),
        cost_estimate=cost(2 * balanced * width * hidden, 2 * width * hidden),
    )(owner, turned, weight, *(() if arrived is None else (arrived,)))


def spread(wide_ref, tenant_ref, ranks_ref, second, scale, tenants, rank):
    balanced, lanes = ranks_ref.shape
    vectors = scale * ranks_ref[...].astype(F32)
    turned = pltpu.roll(vectors, rank, 1)
    high = lax.broadcasted_iota(I32, (balanced, lanes), 1) >= rank
    twice = jnp.where(high, vectors, turned) if second else jnp.where(high, turned, vectors)
    half = (lax.broadcasted_iota(I32, (lanes, balanced), 0) >= rank).astype(F32)
    label = (tenant_ref[0:1, :].astype(F32) - half).T
    for pair in range(tenants // 2):
        wide_ref[:, pair * lanes : (pair + 1) * lanes] = jnp.where(label == 2.0 * pair, twice, 0.0).astype(BF)


def own_and_forward(owners, parts, turned, weight, block):
    balanced, width = parts[0].shape
    hidden = weight.shape[1]
    steps = hidden // block

    def kernel(owners_ref, first_ref, second_ref, turned_ref, mine_ref, other_ref, total_ref, own_ref, sum_ref):
        step = pl.program_id(0)
        piece = jnp.dot(mine_ref[...], turned_ref[...], preferred_element_type=F32)

        @pl.when(step == 0)
        def _():
            sum_ref[...] = piece

        @pl.when(step > 0)
        def _():
            sum_ref[...] += piece

        total_ref[...] = jnp.dot(
            first_ref[...], mine_ref[...], preferred_element_type=F32
        ) + jnp.dot(second_ref[...], other_ref[...], preferred_element_type=F32)

        @pl.when(step == steps - 1)
        def _():
            own_ref[...] = sum_ref[...].T.astype(BF)

    return pl.pallas_call(
        kernel,
        grid_spec=pltpu.PrefetchScalarGridSpec(
            num_scalar_prefetch=1,
            grid=(steps,),
            in_specs=[
                whole((balanced, width)),
                whole((balanced, width)),
                pl.BlockSpec((block, balanced), lambda n, o: (n, 0)),
                pl.BlockSpec((width, block), lambda n, o: (o[0], n)),
                pl.BlockSpec((width, block), lambda n, o: (o[1], n)),
            ],
            out_specs=[pl.BlockSpec((balanced, block), lambda n, o: (0, n)), whole((balanced, width))],
            scratch_shapes=[pltpu.VMEM((width, balanced), F32)],
        ),
        out_shape=[
            jax.ShapeDtypeStruct((balanced, hidden), F32),
            jax.ShapeDtypeStruct((balanced, width), BF),
        ],
        compiler_params=params(),
        cost_estimate=cost(6 * balanced * width * hidden, 4 * width * hidden),
    )(owners, *parts, turned, weight, weight)


def forward(owners, parts, weight, block, total=None, tenant=None, ranks=None, up=None):
    balanced, width = parts[0].shape
    hidden = weight.shape[1]
    count = len(parts)
    last = up is not None

    def kernel(owners_ref, *refs):
        part_refs, weight_refs = refs[:count], refs[count : 2 * count]
        rest = list(refs[2 * count :])
        value = jnp.dot(part_refs[0][...], weight_refs[0][...], preferred_element_type=F32)
        for i in range(1, count):
            value = value + jnp.dot(part_refs[i][...], weight_refs[i][...], preferred_element_type=F32)
        if total is not None:
            value = value + rest.pop(0)[...]
        if last:
            tenant_ref, ranks_ref, up_ref = rest.pop(0), rest.pop(0), rest.pop(0)
            wide_ref = rest.pop()

            @pl.when(pl.program_id(0) == 0)
            def _():
                rank = ranks.shape[1] // 2
                spread(wide_ref, tenant_ref, ranks_ref, False, adapter_scale, up.shape[0] // rank, rank)

            value = value + jnp.dot(wide_ref[...], up_ref[...], preferred_element_type=F32)
        rest[0][...] = value.astype(rest[0].dtype)

    piece = pl.BlockSpec((balanced, block), lambda i, o: (0, i))
    in_specs = [whole((balanced, width))] * count
    for i in range(count):
        in_specs.append(pl.BlockSpec((width, block), lambda n, o, i=i: (o[i], n)))
    operands = [*parts, *([weight] * count)]
    if total is not None:
        in_specs.append(piece)
        operands.append(total)
    if last:
        in_specs += [whole(tenant.shape), whole(ranks.shape), pl.BlockSpec((up.shape[0], block), lambda i, o: (0, i))]
        operands += [tenant, ranks, up]
    return pl.pallas_call(
        kernel,
        grid_spec=pltpu.PrefetchScalarGridSpec(
            num_scalar_prefetch=1,
            grid=(hidden // block,),
            in_specs=in_specs,
            out_specs=piece,
            scratch_shapes=[pltpu.VMEM((balanced, up.shape[0]), BF)] if last else [],
        ),
        out_shape=jax.ShapeDtypeStruct((balanced, hidden), BF if last else F32),
        compiler_params=params(),
        cost_estimate=cost(
            2 * balanced * hidden * (count * width + (up.shape[0] if last else 0)),
            2 * hidden * (count * width + (up.shape[0] if last else 0)),
        ),
    )(owners, *operands)


def finish_gradient(terms, tenant, ranks, down, block):
    balanced, width = terms[0].shape

    lanes = ranks.shape[1]
    rank = lanes // 2

    def kernel(tenant_ref, ranks_ref, down_ref, *refs):
        term_refs, out_ref, wide_ref = refs[:-2], refs[-2], refs[-1]
        spread(wide_ref, tenant_ref, ranks_ref, True, 1.0, down.shape[0] // rank, rank)
        for start in range(0, width, block):
            at = pl.ds(start, block)
            value = jnp.dot(wide_ref[...], down_ref[:, at], preferred_element_type=F32)
            for term_ref in term_refs:
                value = value + term_ref[:, at].astype(F32)
            out_ref[:, at] = value.astype(BF)
        out_ref[:, pl.ds(width, lanes)] = ranks_ref[...]

    return pl.pallas_call(
        kernel,
        grid=(1,),
        in_specs=[whole(tenant.shape), whole(ranks.shape), whole(down.shape)] + [whole((balanced, width))] * len(terms),
        out_specs=whole((balanced, width + lanes)),
        out_shape=jax.ShapeDtypeStruct((balanced, width + lanes), BF),
        scratch_shapes=[pltpu.VMEM((balanced, down.shape[0]), BF)],
        compiler_params=params(),
        cost_estimate=cost(2 * balanced * down.size, 2 * down.size),
    )(tenant, ranks, down, *terms)


def owned_gradient(place, slot, bundles, second, values, share, lanes, scale, block):
    groups, balanced = slot.shape
    rank = lanes // 2
    width = values[0].shape[1]
    column = bundles[0].shape[1] // lanes - 1

    def kernel(place_ref, slot_ref, *refs):
        rank_refs, value_refs = refs[:groups], refs[groups : 2 * groups]
        out_ref, wide_ref = refs[2 * groups :]

        @pl.when(pl.program_id(0) == 0)
        def _():
            first = place_ref[0] * share
            for k in range(groups):
                turned = rank_refs[k][...].astype(F32).T
                mine = turned[rank:, :] if second else turned[:rank, :]
                for s in range(share):
                    wide_ref[k, s * rank : (s + 1) * rank, :] = jnp.where(
                        slot_ref[k : k + 1, :] == first + s, mine, 0.0
                    ).astype(BF)

        value = jnp.dot(wide_ref[0], value_refs[0][...], preferred_element_type=F32)
        for k in range(1, groups):
            value = value + jnp.dot(wide_ref[k], value_refs[k][...], preferred_element_type=F32)
        out_ref[...] = (scale * value).astype(BF)

    return pl.pallas_call(
        kernel,
        grid=(width // block,),
        in_specs=[SMEM(), whole(slot.shape)]
        + [pl.BlockSpec((balanced, lanes), lambda i: (0, column))] * groups
        + [pl.BlockSpec((balanced, block), lambda i: (0, i))] * groups,
        out_specs=pl.BlockSpec((share * rank, block), lambda i: (0, i)),
        out_shape=jax.ShapeDtypeStruct((share * rank, width), BF),
        scratch_shapes=[pltpu.VMEM((groups, share * rank, balanced), BF)],
        compiler_params=params(),
        cost_estimate=cost(2 * groups * balanced * share * rank * width, 2 * width * (groups * balanced + share * rank)),
    )(place, slot, *bundles, *values)


def bring_home(place, handoff, bundles, capacity, width):
    balanced = bundles[0].shape[0]
    groups = handoff.shape[0]

    def kernel(place_ref, handoff_ref, *refs):
        out_ref = refs[-1]
        mine = place_ref[0]
        row = lax.broadcasted_iota(I32, (capacity, balanced), 0)
        here = lax.broadcasted_iota(I32, (capacity, balanced), 1)
        total = jnp.zeros((capacity, width), F32)
        for k in range(groups):
            taker = mine ^ k
            sent, got = before(handoff_ref, mine, taker, groups)
            inside = (row >= sent) & (row < sent + handoff_ref[mine, taker])
            pick = inside & (here == row - sent + got)
            total = total + jnp.dot(pick.astype(F32).astype(BF), refs[k][...], preferred_element_type=F32)
        out_ref[...] = total.astype(BF)

    return pl.pallas_call(
        kernel,
        grid=(1,),
        in_specs=[SMEM(), SMEM()] + [whole((balanced, width))] * groups,
        out_specs=whole((capacity, width)),
        out_shape=jax.ShapeDtypeStruct((capacity, width), BF),
        compiler_params=params(),
        cost_estimate=cost(2 * groups * balanced * capacity * width, 4 * groups * balanced * width),
    )(place, handoff, *bundles)


def swap(values, axis, distance):
    size = lax.axis_size(axis)
    return lax.ppermute(values, axis, [(i, i ^ distance) for i in range(size)])


def after(values, *earlier):
    return lax.optimization_barrier((values, *earlier))[0]


def fast_body(
    input_rows,
    cotangent,
    frozen_weight,
    adapter_down_weight,
    adapter_up_weight,
    tenant_row_counts,
    handoff_counts,
    tenant_gradient_slot,
):
    mine = lax.axis_index("dp")
    z = lax.axis_index("fsdp")
    balanced = cotangent.shape[0]
    capacity, width = input_rows.shape
    tenants, rank, hidden = adapter_up_weight.shape
    share = tenants // lax.axis_size("dp")
    place = mine.astype(I32).reshape(1)
    owner = [(z ^ k).astype(I32) for k in range(4)]
    down = adapter_down_weight.transpose(0, 2, 1).reshape(tenants * rank, width)
    up = adapter_up_weight.reshape(tenants * rank, hidden)
    turned = cotangent.T

    *outgoing, tenant, slot = pack(
        place, handoff_counts, tenant_row_counts, tenant_gradient_slot, input_rows, balanced, balanced // 2
    )
    arrived = [None] * 3
    for k in (2, 3, 1):
        arrived[k - 1] = swap(outgoing[k - 1], "dp", k)
    far = base_gradient(owner[3].reshape(1), after(turned, *outgoing), frozen_weight, width, 512)
    for_far = swap(far, "fsdp", 1)
    near = base_gradient(owner[1].reshape(1), turned, after(frozen_weight, far), width, 512)
    from_near = swap(near, "fsdp", 1)
    gathered, lowered = unpack(
        place, handoff_counts, tenant, input_rows, arrived, after(down, near, *arrived), rank, 512
    )
    beside = swap(gathered, "fsdp", 1)
    pair = swap(gathered, "fsdp", 2)
    cot_x = swap(after(cotangent, *arrived, far), "dp", 2)
    partial = rank_backward(tenant, turned, after(up, gathered, for_far), lowered, 512)
    across = base_gradient(
        owner[2].reshape(1), turned, after(frozen_weight, partial), width, 512, for_far
    )
    late = after(partial, across, cot_x, from_near)
    sums = [swap(late, "fsdp", k) for k in (1, 2, 3)]
    from_pair = swap(after(across, from_near, cot_x), "fsdp", 2)
    total, own = own_and_forward(
        jnp.stack([owner[0], owner[1]]), [gathered, beside], turned, after(frozen_weight, across), 512
    )
    diagonal = swap(after(pair, total), "fsdp", 1)
    gathered_x = swap(after(gathered, total), "dp", 2)
    scale = jnp.where(jnp.arange(2 * rank) < rank, 1.0, adapter_scale).astype(F32)
    ranks = ((after(partial, total, from_pair) + sums[0] + (sums[1] + sums[2])) * scale).astype(BF)
    bundle = finish_gradient([own, from_near, from_pair], tenant, ranks, after(down, total), 512)
    bundle_x = swap(bundle, "dp", 2)
    bundle_c = swap(bundle, "dp", 1)
    cot_all = [
        cotangent,
        swap(after(cotangent, bundle), "dp", 1),
        cot_x,
        swap(after(cot_x, bundle), "dp", 1),
    ]
    outputs = forward(
        jnp.stack([owner[2], owner[3]]),
        [pair, diagonal],
        after(frozen_weight, bundle, diagonal),
        512,
        total,
        tenant,
        ranks,
        up,
    )
    bundles = [bundle, bundle_c, bundle_x, swap(after(bundle_x, outputs), "dp", 1)]
    gathered_all = [
        gathered,
        swap(after(gathered, outputs), "dp", 1),
        gathered_x,
        swap(after(gathered_x, outputs), "dp", 1),
    ]
    grad_b = owned_gradient(
        place, slot, after(bundles, outputs), False, cot_all, share, 2 * rank, adapter_scale, 1024
    )
    grad_a = owned_gradient(
        place, slot, after(bundles, grad_b), True, gathered_all, share, 2 * rank, 1.0, 512
    )
    row_grad = bring_home(place, handoff_counts, after(bundles, grad_a), capacity, width)
    return (
        outputs,
        row_grad,
        grad_a.reshape(share, rank, width).transpose(0, 2, 1),
        grad_b.reshape(share, rank, hidden),
    )


def solution(mesh):
    placed = (
        P(("groups", "dp"), "fsdp"),
        P(("groups", "dp"), "fsdp"),
        P(None, "fsdp"),
        P("groups", "fsdp", None),
        P("groups", None, "fsdp"),
        P("groups", None),
        P("groups", None),
        P("groups"),
    )
    four_by_four = mesh.shape["dp"] == 4 and mesh.shape["fsdp"] == 4
    return jax.shard_map(
        fast_body if four_by_four else plain_body,
        mesh=mesh,
        in_specs=placed,
        out_specs=(
            P(("groups", "dp"), "fsdp"),
            P(("groups", "dp"), "fsdp"),
            P(("groups", "dp"), "fsdp", None),
            P(("groups", "dp"), None, "fsdp"),
        ),
        check_vma=False,
    )
```

```python
import functools

import jax
import jax.numpy as jnp
from jax import lax
from jax.experimental import pallas as pl
from jax.experimental.pallas import tpu as pltpu
from jax.sharding import PartitionSpec as P

adapter_scale = 0.25
BF = jnp.bfloat16
F32 = jnp.float32
I32 = jnp.int32
VMEM_LIMIT = 32 * 2**20


def before_sums(values, group_axis):
    return jnp.cumsum(values, axis=group_axis) - values


def find_source(starts, counts, length):
    places = jnp.arange(length, dtype=jnp.int32)[:, None]
    inside = (places >= starts[None, :]) & (places < (starts + counts)[None, :])
    numbers = jnp.arange(starts.shape[0], dtype=jnp.int32)[None, :]
    source = jnp.sum(jnp.where(inside, numbers, 0), axis=1)
    offset = places[:, 0] - jnp.sum(jnp.where(inside, starts[None, :], 0), axis=1)
    present = jnp.any(inside, axis=1)
    return (source, offset, present)


def pack_slots(values, starts, counts, width, allowed):
    places = jnp.arange(width, dtype=jnp.int32)[None, :]
    picked = jnp.minimum(starts[:, None] + places, values.shape[0] - 1)
    valid = (places < counts[:, None]) & allowed[:, None]
    taken = jnp.take(values, picked.reshape(-1), axis=0).reshape(
        counts.shape[0], width, values.shape[1]
    )
    return jnp.where(valid[:, :, None], taken, jnp.zeros((), values.dtype))


def plain_body(
    input_rows,
    cotangent,
    frozen_weight,
    adapter_down_weight,
    adapter_up_weight,
    tenant_row_counts,
    handoff_counts,
    tenant_gradient_slot,
):
    groups = lax.axis_size("dp")
    mine = lax.axis_index("dp")
    balanced_rows = cotangent.shape[0]
    capacity = input_rows.shape[0]
    feature_width = input_rows.shape[1]
    column_index = cotangent.shape[1]
    tenant_labels = adapter_up_weight.shape[0]
    group_position = adapter_up_weight.shape[1]
    sent_before = before_sums(handoff_counts, 1)
    recv_before = before_sums(handoff_counts, 0)
    my_sends = handoff_counts[mine]
    my_send_starts = sent_before[mine]
    my_recvs = handoff_counts[:, mine]
    my_recv_starts = recv_before[:, mine]
    others = jnp.arange(groups, dtype=jnp.int32) != mine
    source, offset, present = find_source(my_recv_starts, my_recvs, balanced_rows)
    source_row = sent_before[source, mine] + offset
    tenant_end = jnp.cumsum(tenant_row_counts, axis=1)
    row_tenant = jnp.sum(
        (jnp.take(tenant_end, source, axis=0) <= source_row[:, None]).astype(jnp.int32), axis=1
    )
    tenant_onehot = (
        row_tenant[:, None] == jnp.arange(tenant_labels, dtype=jnp.int32)[None, :]
    ).astype(jnp.bfloat16)
    half_slot = balanced_rows // 2
    outgoing = pack_slots(input_rows, my_send_starts, my_sends, half_slot, others)
    arrived = lax.all_to_all(outgoing, "dp", split_axis=0, concat_axis=0, tiled=True)
    pool = jnp.concatenate([arrived.reshape(groups * half_slot, feature_width), input_rows], axis=0)
    picked = jnp.where(source == mine, groups * half_slot + source_row, source * half_slot + offset)
    group_rows = jnp.take(pool, jnp.minimum(picked, pool.shape[0] - 1), axis=0)
    frozen_output = jnp.dot(
        lax.all_gather(group_rows, "fsdp", axis=1, tiled=True),
        frozen_weight,
        preferred_element_type=jnp.float32,
    )
    lowered_gathered = jnp.einsum(
        "ai,wiv->awv", group_rows, adapter_down_weight, preferred_element_type=jnp.float32
    )
    backward_gathered = jnp.einsum(
        "ku,wxu->kwx", cotangent, adapter_up_weight, preferred_element_type=jnp.float32
    )
    hot_wide = tenant_onehot.astype(jnp.float32)[:, :, None]
    down_part = jnp.sum(lowered_gathered * hot_wide, axis=1)
    back_part = jnp.sum(backward_gathered * hot_wide, axis=1)
    lowered_total, backward_total = lax.psum((down_part, back_part), "fsdp")
    adapter_input = lowered_total.astype(jnp.bfloat16)
    adapter_gradient = (adapter_scale * backward_total).astype(jnp.bfloat16)
    scattered_input = (tenant_onehot[:, :, None] * adapter_input[:, None, :]).reshape(
        balanced_rows, tenant_labels * group_position
    )
    scattered_gradient = (tenant_onehot[:, :, None] * adapter_gradient[:, None, :]).reshape(
        balanced_rows, tenant_labels * group_position
    )
    adapter_output = jnp.dot(
        scattered_input,
        adapter_up_weight.reshape(tenant_labels * group_position, column_index),
        preferred_element_type=jnp.float32,
    )
    adapter_backward = lax.dot_general(
        scattered_gradient,
        adapter_down_weight.transpose(1, 0, 2).reshape(
            feature_width, tenant_labels * group_position
        ),
        (((1,), (1,)), ((), ())),
        preferred_element_type=jnp.float32,
    )
    outputs = (frozen_output + adapter_scale * adapter_output).astype(jnp.bfloat16)
    grad_terms = lax.dot_general(
        cotangent, frozen_weight, (((1,), (1,)), ((), ())), preferred_element_type=jnp.float32
    )
    frozen_gradient = lax.psum_scatter(grad_terms, "fsdp", scatter_dimension=1, tiled=True)
    group_gradient = (frozen_gradient + adapter_backward).astype(jnp.bfloat16)
    part_a = lax.dot_general(
        group_rows, scattered_gradient, (((0,), (0,)), ((), ())), preferred_element_type=jnp.float32
    )
    part_a = part_a.reshape(feature_width, tenant_labels, group_position).transpose(1, 0, 2)
    partial_up = adapter_scale * lax.dot_general(
        scattered_input, cotangent, (((0,), (0,)), ((), ())), preferred_element_type=jnp.float32
    )
    partial_up = partial_up.reshape(tenant_labels, group_position, column_index)
    order = jnp.argsort(tenant_gradient_slot)
    share = tenant_labels // groups
    owner_a = (
        jnp.take(part_a, order, axis=0)
        .astype(jnp.bfloat16)
        .reshape(groups, share, feature_width, group_position)
    )
    owner_b = (
        jnp.take(partial_up, order, axis=0)
        .astype(jnp.bfloat16)
        .reshape(groups, share, group_position, column_index)
    )
    source_home, offset_home, present_home = find_source(my_send_starts, my_sends, capacity)
    half_slot = balanced_rows // 2
    back_slots = pack_slots(group_gradient, my_recv_starts, my_recvs, half_slot, others)
    home, sums_a, sums_b = (
        lax.all_to_all(back_slots, "dp", split_axis=0, concat_axis=0, tiled=True),
        lax.all_to_all(owner_a, "dp", split_axis=0, concat_axis=0, tiled=True),
        lax.all_to_all(owner_b, "dp", split_axis=0, concat_axis=0, tiled=True),
    )
    pool_home = jnp.concatenate(
        [home.reshape(groups * half_slot, feature_width), group_gradient], axis=0
    )
    picked_home = jnp.where(
        source_home == mine,
        groups * half_slot + recv_before[mine, mine] + offset_home,
        source_home * half_slot + offset_home,
    )
    row_grad = jnp.take(pool_home, jnp.minimum(picked_home, pool_home.shape[0] - 1), axis=0)
    row_grad = jnp.where(present_home[:, None], row_grad, jnp.zeros((), jnp.bfloat16))
    grad_a = jnp.sum(sums_a.astype(jnp.float32), axis=0).astype(jnp.bfloat16)
    grad_b = jnp.sum(sums_b.astype(jnp.float32), axis=0).astype(jnp.bfloat16)
    return (outputs, row_grad, grad_a, grad_b)


def params(limit=VMEM_LIMIT):
    return pltpu.CompilerParams(vmem_limit_bytes=limit)


def cost(flops, moved):
    return pl.CostEstimate(flops=int(flops) // 1000, bytes_accessed=int(moved) // 1000, transcendentals=0)


SMEM = functools.partial(pl.BlockSpec, memory_space=pltpu.SMEM)


def whole(shape):
    return pl.BlockSpec(shape, lambda *_: (0,) * len(shape))


def before(handoff_ref, giver, taker, groups):
    sent = jnp.int32(0)
    got = jnp.int32(0)
    for other in range(groups):
        sent = sent + jnp.where(other < taker, handoff_ref[giver, other], 0)
        got = got + jnp.where(other < giver, handoff_ref[other, taker], 0)
    return sent, got


def pack(place, handoff, counts, slots, rows, balanced, half):
    groups, tenants = counts.shape
    capacity, width = rows.shape

    def kernel(place_ref, handoff_ref, slots_ref, counts_ref, rows_ref, *outs):
        out_refs, tenant_ref, slot_ref = outs[: groups - 1], outs[groups - 1], outs[groups]
        mine = place_ref[0]
        here = lax.broadcasted_iota(I32, (half, capacity), 1)
        slot = lax.broadcasted_iota(I32, (half, capacity), 0)
        for step in range(1, groups):
            partner = mine ^ step
            sent, _ = before(handoff_ref, mine, partner, groups)
            pick = (here == slot + sent) & (slot < handoff_ref[mine, partner])
            out_refs[step - 1][...] = jnp.dot(
                pick.astype(F32).astype(BF), rows_ref[...], preferred_element_type=F32
            ).astype(BF)
        upto = lax.broadcasted_iota(I32, (tenants, tenants), 1) <= lax.broadcasted_iota(
            I32, (tenants, tenants), 0
        )
        ends = lax.dot_general(
            upto.astype(F32).astype(BF),
            counts_ref[...].astype(F32).astype(BF),
            (((1,), (1,)), ((), ())),
            preferred_element_type=F32,
        ).astype(I32)
        place_of = lax.broadcasted_iota(I32, (1, balanced), 1)
        for step in range(groups):
            taker = mine ^ step
            position = place_of
            row_ends = jnp.zeros((tenants, balanced), I32)
            for giver in range(groups):
                sent, got = before(handoff_ref, giver, taker, groups)
                inside = (place_of >= got) & (place_of < got + handoff_ref[giver, taker])
                position = position + jnp.where(inside, sent - got, 0)
                row_ends = row_ends + jnp.where(inside, ends[:, giver : giver + 1], 0)
            tenant = jnp.sum((row_ends <= position).astype(I32), axis=0, keepdims=True)
            target = jnp.zeros((1, balanced), I32)
            for label in range(tenants):
                target = target + jnp.where(tenant == label, slots_ref[label], 0)
            tenant_ref[step : step + 1, :] = tenant
            slot_ref[step : step + 1, :] = target

    return pl.pallas_call(
        kernel,
        in_specs=[SMEM(), SMEM(), SMEM(), pl.BlockSpec(memory_space=pltpu.VMEM), pl.BlockSpec(memory_space=pltpu.VMEM)],
        out_shape=[jax.ShapeDtypeStruct((half, width), BF)] * (groups - 1)
        + [jax.ShapeDtypeStruct((groups, balanced), I32)] * 2,
        compiler_params=params(60 * 2**20),
        cost_estimate=cost(2 * 3 * half * capacity * width, 2 * capacity * width * 2),
    )(place, handoff, slots, counts, rows)


def masked_rank(product, tenant, first, rank):
    total = jnp.zeros((rank, product.shape[1]), F32)
    for label in range(product.shape[0] // rank):
        total = total + jnp.where(tenant == first + label, product[label * rank : (label + 1) * rank], 0.0)
    return total


def unpack(place, handoff, tenant, rows, arrived, down, rank, block):
    groups, balanced = tenant.shape
    capacity, width = rows.shape
    half = arrived[0].shape[0]

    def kernel(place_ref, handoff_ref, tenant_ref, rows_ref, *refs):
        arrived_refs = refs[: groups - 1]
        down_ref, gathered_ref, lowered_ref, turned = refs[groups - 1 :]
        step = pl.program_id(0)

        @pl.when(step == 0)
        def _():
            mine = place_ref[0]
            place_of = lax.broadcasted_iota(I32, (balanced, capacity), 0)
            here = lax.broadcasted_iota(I32, (balanced, capacity), 1)
            sent, got = before(handoff_ref, mine, mine, groups)
            inside = (place_of >= got) & (place_of < got + handoff_ref[mine, mine])
            pick = inside & (here == place_of - got + sent)
            total = jnp.dot(pick.astype(F32).astype(BF), rows_ref[...], preferred_element_type=F32)
            place_of = lax.broadcasted_iota(I32, (balanced, half), 0)
            here = lax.broadcasted_iota(I32, (balanced, half), 1)
            for k in range(1, groups):
                giver = mine ^ k
                _, got = before(handoff_ref, giver, mine, groups)
                inside = (place_of >= got) & (place_of < got + handoff_ref[giver, mine])
                pick = inside & (here == place_of - got)
                total = total + jnp.dot(
                    pick.astype(F32).astype(BF), arrived_refs[k - 1][...], preferred_element_type=F32
                )
            gathered_ref[...] = total.astype(BF)
            turned[...] = total.T.astype(BF)
            lowered_ref[...] = jnp.zeros_like(lowered_ref)

        product = jnp.dot(down_ref[...], turned[...], preferred_element_type=F32)
        lowered_ref[...] += masked_rank(product, tenant_ref[0:1, :], step * (block // rank), rank)

    return pl.pallas_call(
        kernel,
        grid=(down.shape[0] // block,),
        in_specs=[SMEM(), SMEM(), whole((groups, balanced)), whole((capacity, width))]
        + [whole((half, width))] * (groups - 1)
        + [pl.BlockSpec((block, width), lambda i: (i, 0))],
        out_specs=[whole((balanced, width)), whole((rank, balanced))],
        out_shape=[
            jax.ShapeDtypeStruct((balanced, width), BF),
            jax.ShapeDtypeStruct((rank, balanced), F32),
        ],
        scratch_shapes=[pltpu.VMEM((width, balanced), BF)],
        compiler_params=params(),
        cost_estimate=cost(2 * balanced * down.size, 2 * down.size + 6 * balanced * width),
    )(place, handoff, tenant, rows, *arrived, down)


def rank_backward(tenant, turned, up, lowered, block):
    rank, balanced = lowered.shape
    hidden = up.shape[1]
    steps = up.shape[0] // block

    def kernel(tenant_ref, turned_ref, lowered_ref, up_ref, out_ref, total_ref):
        step = pl.program_id(0)

        @pl.when(step == 0)
        def _():
            total_ref[:rank, :] = lowered_ref[...]
            total_ref[rank:, :] = jnp.zeros((rank, balanced), F32)

        product = jnp.dot(up_ref[...], turned_ref[...], preferred_element_type=F32)
        total_ref[rank:, :] += masked_rank(product, tenant_ref[0:1, :], step * (block // rank), rank)

        @pl.when(step == steps - 1)
        def _():
            out_ref[...] = total_ref[...].T

    return pl.pallas_call(
        kernel,
        grid=(steps,),
        in_specs=[
            whole(tenant.shape), whole(turned.shape), whole(lowered.shape),
            pl.BlockSpec((block, hidden), lambda i: (i, 0)),
        ],
        out_specs=whole((balanced, 2 * rank)),
        out_shape=jax.ShapeDtypeStruct((balanced, 2 * rank), F32),
        scratch_shapes=[pltpu.VMEM((2 * rank, balanced), F32)],
        compiler_params=params(50 * 2**20),
        cost_estimate=cost(2 * balanced * up.size, 2 * up.size),
    )(tenant, turned, lowered, up)


def base_gradient(owner, turned, weight, width, block, arrived=None):
    hidden, balanced = turned.shape
    steps = width // block

    def kernel(owner_ref, turned_ref, weight_ref, *refs):
        product = jnp.dot(weight_ref[...], turned_ref[...], preferred_element_type=F32).T
        if arrived is not None:
            product = product + refs[0][...].astype(F32)
        refs[-1][...] = product.astype(BF)

    piece = pl.BlockSpec((balanced, block), lambda i, owner_ref: (0, i))
    return pl.pallas_call(
        kernel,
        grid_spec=pltpu.PrefetchScalarGridSpec(
            num_scalar_prefetch=1,
            grid=(steps,),
            in_specs=[
                whole(turned.shape),
                pl.BlockSpec((block, hidden), lambda i, owner_ref: (owner_ref[0] * steps + i, 0)),
            ]
            + ([] if arrived is None else [piece]),
            out_specs=piece,
        ),
        out_shape=jax.ShapeDtypeStruct((balanced, width), BF),
        compiler_params=params(),
        cost_estimate=cost(2 * balanced * width * hidden, 2 * width * hidden),
    )(owner, turned, weight, *(() if arrived is None else (arrived,)))


def turn_and_far(owner, cotangent, weight, width, block):
    balanced, hidden = cotangent.shape
    steps = width // block

    def kernel(owner_ref, cotangent_ref, weight_ref, far_ref, turned_ref):
        @pl.when(pl.program_id(0) == 0)
        def _():
            turned_ref[...] = cotangent_ref[...].astype(F32).T.astype(BF)

        far_ref[...] = jnp.dot(weight_ref[...], turned_ref[...], preferred_element_type=F32).T.astype(BF)

    return pl.pallas_call(
        kernel,
        grid_spec=pltpu.PrefetchScalarGridSpec(
            num_scalar_prefetch=1,
            grid=(steps,),
            in_specs=[
                whole(cotangent.shape),
                pl.BlockSpec((block, hidden), lambda i, o: (o[0] * steps + i, 0)),
            ],
            out_specs=[pl.BlockSpec((balanced, block), lambda i, o: (0, i)), whole((hidden, balanced))],
        ),
        out_shape=[
            jax.ShapeDtypeStruct((balanced, width), BF),
            jax.ShapeDtypeStruct((hidden, balanced), BF),
        ],
        compiler_params=params(),
        cost_estimate=cost(2 * balanced * width * hidden, 2 * width * hidden),
    )(owner, cotangent, weight)


def spread(wide_ref, tenant_ref, ranks_ref, second, scale, tenants, rank):
    balanced, lanes = ranks_ref.shape
    vectors = scale * ranks_ref[...].astype(F32)
    turned = pltpu.roll(vectors, rank, 1)
    high = lax.broadcasted_iota(I32, (balanced, lanes), 1) >= rank
    twice = jnp.where(high, vectors, turned) if second else jnp.where(high, turned, vectors)
    half = (lax.broadcasted_iota(I32, (lanes, balanced), 0) >= rank).astype(F32)
    label = (tenant_ref[0:1, :].astype(F32) - half).T
    for pair in range(tenants // 2):
        wide_ref[:, pair * lanes : (pair + 1) * lanes] = jnp.where(label == 2.0 * pair, twice, 0.0).astype(BF)


def own_and_forward(owner, part, turned, weight, block):
    balanced, width = part.shape
    hidden = weight.shape[1]
    steps = width // block

    def kernel(owner_ref, part_ref, turned_ref, weight_ref, total_ref, own_ref):
        own_ref[...] = jnp.dot(weight_ref[...], turned_ref[...], preferred_element_type=F32).T.astype(BF)
        piece = jnp.dot(part_ref[...], weight_ref[...], preferred_element_type=F32)

        @pl.when(pl.program_id(0) == 0)
        def _():
            total_ref[...] = piece

        @pl.when(pl.program_id(0) > 0)
        def _():
            total_ref[...] += piece

    columns = pl.BlockSpec((balanced, block), lambda i, o: (0, i))
    return pl.pallas_call(
        kernel,
        grid_spec=pltpu.PrefetchScalarGridSpec(
            num_scalar_prefetch=1,
            grid=(steps,),
            in_specs=[
                columns,
                whole(turned.shape),
                pl.BlockSpec((block, hidden), lambda i, o: (o[0] * steps + i, 0)),
            ],
            out_specs=[whole((balanced, hidden)), columns],
        ),
        out_shape=[
            jax.ShapeDtypeStruct((balanced, hidden), F32),
            jax.ShapeDtypeStruct((balanced, width), BF),
        ],
        compiler_params=params(),
        cost_estimate=cost(4 * balanced * width * hidden, 2 * width * hidden),
    )(owner, part, turned, weight)


def forward(owners, parts, weight, block, total=None, tenant=None, ranks=None, up=None):
    balanced, width = parts[0].shape
    hidden = weight.shape[1]
    count = len(parts)
    last = up is not None

    def kernel(owners_ref, *refs):
        part_refs, weight_refs = refs[:count], refs[count : 2 * count]
        rest = list(refs[2 * count :])
        value = jnp.dot(part_refs[0][...], weight_refs[0][...], preferred_element_type=F32)
        for i in range(1, count):
            value = value + jnp.dot(part_refs[i][...], weight_refs[i][...], preferred_element_type=F32)
        if total is not None:
            value = value + rest.pop(0)[...]
        if last:
            tenant_ref, ranks_ref, up_ref = rest.pop(0), rest.pop(0), rest.pop(0)
            wide_ref = rest.pop()

            @pl.when(pl.program_id(0) == 0)
            def _():
                rank = ranks.shape[1] // 2
                spread(wide_ref, tenant_ref, ranks_ref, False, adapter_scale, up.shape[0] // rank, rank)

            value = value + jnp.dot(wide_ref[...], up_ref[...], preferred_element_type=F32)
        rest[0][...] = value.astype(rest[0].dtype)

    piece = pl.BlockSpec((balanced, block), lambda i, o: (0, i))
    in_specs = [whole((balanced, width))] * count
    for i in range(count):
        in_specs.append(pl.BlockSpec((width, block), lambda n, o, i=i: (o[i], n)))
    operands = [*parts, *([weight] * count)]
    if total is not None:
        in_specs.append(piece)
        operands.append(total)
    if last:
        in_specs += [whole(tenant.shape), whole(ranks.shape), pl.BlockSpec((up.shape[0], block), lambda i, o: (0, i))]
        operands += [tenant, ranks, up]
    return pl.pallas_call(
        kernel,
        grid_spec=pltpu.PrefetchScalarGridSpec(
            num_scalar_prefetch=1,
            grid=(hidden // block,),
            in_specs=in_specs,
            out_specs=piece,
            scratch_shapes=[pltpu.VMEM((balanced, up.shape[0]), BF)] if last else [],
        ),
        out_shape=jax.ShapeDtypeStruct((balanced, hidden), BF if last else F32),
        compiler_params=params(50 * 2**20 if last else VMEM_LIMIT),
        cost_estimate=cost(
            2 * balanced * hidden * (count * width + (up.shape[0] if last else 0)),
            2 * hidden * (count * width + (up.shape[0] if last else 0)),
        ),
    )(owners, *operands)


def finish_gradient(terms, tenant, ranks, down, block):
    balanced, width = terms[0].shape

    lanes = ranks.shape[1]
    rank = lanes // 2

    def kernel(tenant_ref, ranks_ref, down_ref, *refs):
        term_refs, out_ref, wide_ref = refs[:-2], refs[-2], refs[-1]
        spread(wide_ref, tenant_ref, ranks_ref, True, 1.0, down.shape[0] // rank, rank)
        for start in range(0, width, block):
            at = pl.ds(start, block)
            value = jnp.dot(wide_ref[...], down_ref[:, at], preferred_element_type=F32)
            for term_ref in term_refs:
                value = value + term_ref[:, at].astype(F32)
            out_ref[:, at] = value.astype(BF)
        out_ref[:, pl.ds(width, lanes)] = ranks_ref[...]

    return pl.pallas_call(
        kernel,
        grid=(1,),
        in_specs=[whole(tenant.shape), whole(ranks.shape), whole(down.shape)] + [whole((balanced, width))] * len(terms),
        out_specs=whole((balanced, width + lanes)),
        out_shape=jax.ShapeDtypeStruct((balanced, width + lanes), BF),
        scratch_shapes=[pltpu.VMEM((balanced, down.shape[0]), BF)],
        compiler_params=params(),
        cost_estimate=cost(2 * balanced * down.size, 2 * down.size),
    )(tenant, ranks, down, *terms)


def owned_gradient(place, slot, bundles, second, values, share, lanes, scale, block):
    groups, balanced = slot.shape
    rank = lanes // 2
    width = values[0].shape[1]
    column = bundles[0].shape[1] // lanes - 1

    def kernel(place_ref, slot_ref, *refs):
        rank_refs, value_refs = refs[:groups], refs[groups : 2 * groups]
        out_ref, wide_ref = refs[2 * groups :]

        @pl.when(pl.program_id(0) == 0)
        def _():
            first = place_ref[0] * share
            for k in range(groups):
                turned = rank_refs[k][...].astype(F32).T
                mine = turned[rank:, :] if second else turned[:rank, :]
                for s in range(share):
                    wide_ref[k, s * rank : (s + 1) * rank, :] = jnp.where(
                        slot_ref[k : k + 1, :] == first + s, mine, 0.0
                    ).astype(BF)

        value = jnp.dot(wide_ref[0], value_refs[0][...], preferred_element_type=F32)
        for k in range(1, groups):
            value = value + jnp.dot(wide_ref[k], value_refs[k][...], preferred_element_type=F32)
        out_ref[...] = (scale * value).astype(BF)

    return pl.pallas_call(
        kernel,
        grid=(width // block,),
        in_specs=[SMEM(), whole(slot.shape)]
        + [pl.BlockSpec((balanced, lanes), lambda i: (0, column))] * groups
        + [pl.BlockSpec((balanced, block), lambda i: (0, i))] * groups,
        out_specs=pl.BlockSpec((share * rank, block), lambda i: (0, i)),
        out_shape=jax.ShapeDtypeStruct((share * rank, width), BF),
        scratch_shapes=[pltpu.VMEM((groups, share * rank, balanced), BF)],
        compiler_params=params(),
        cost_estimate=cost(2 * groups * balanced * share * rank * width, 2 * width * (groups * balanced + share * rank)),
    )(place, slot, *bundles, *values)


def bring_home(place, handoff, bundles, capacity, width):
    balanced = bundles[0].shape[0]
    groups = handoff.shape[0]

    def kernel(place_ref, handoff_ref, *refs):
        out_ref = refs[-1]
        mine = place_ref[0]
        row = lax.broadcasted_iota(I32, (capacity, balanced), 0)
        here = lax.broadcasted_iota(I32, (capacity, balanced), 1)
        total = jnp.zeros((capacity, width), F32)
        for k in range(groups):
            taker = mine ^ k
            sent, got = before(handoff_ref, mine, taker, groups)
            inside = (row >= sent) & (row < sent + handoff_ref[mine, taker])
            pick = inside & (here == row - sent + got)
            total = total + jnp.dot(pick.astype(F32).astype(BF), refs[k][...], preferred_element_type=F32)
        out_ref[...] = total.astype(BF)

    return pl.pallas_call(
        kernel,
        grid=(1,),
        in_specs=[SMEM(), SMEM()] + [whole((balanced, width))] * groups,
        out_specs=whole((capacity, width)),
        out_shape=jax.ShapeDtypeStruct((capacity, width), BF),
        compiler_params=params(),
        cost_estimate=cost(2 * groups * balanced * capacity * width, 4 * groups * balanced * width),
    )(place, handoff, *bundles)


def swap(values, axis, distance):
    size = lax.axis_size(axis)
    return lax.ppermute(values, axis, [(i, i ^ distance) for i in range(size)])


def after(values, *earlier):
    return lax.optimization_barrier((values, *earlier))[0]


def fast_body(
    input_rows,
    cotangent,
    frozen_weight,
    adapter_down_weight,
    adapter_up_weight,
    tenant_row_counts,
    handoff_counts,
    tenant_gradient_slot,
):
    mine = lax.axis_index("dp")
    z = lax.axis_index("fsdp")
    balanced = cotangent.shape[0]
    capacity, width = input_rows.shape
    tenants, rank, hidden = adapter_up_weight.shape
    share = tenants // lax.axis_size("dp")
    place = mine.astype(I32).reshape(1)
    owner = [(z ^ k).astype(I32) for k in range(4)]
    down = adapter_down_weight.transpose(0, 2, 1).reshape(tenants * rank, width)
    up = adapter_up_weight.reshape(tenants * rank, hidden)

    *outgoing, tenant, slot = pack(
        place, handoff_counts, tenant_row_counts, tenant_gradient_slot, input_rows, balanced, balanced // 2
    )
    arrived = [None] * 3
    for k in (2, 3, 1):
        arrived[k - 1] = swap(outgoing[k - 1], "dp", k)
    far, turned = turn_and_far(
        owner[3].reshape(1), cotangent, after(frozen_weight, tenant), width, 512
    )
    for_far = swap(far, "fsdp", 1)
    near = base_gradient(owner[1].reshape(1), turned, after(frozen_weight, far), width, 512)
    from_near = swap(near, "fsdp", 1)
    gathered, lowered = unpack(
        place, handoff_counts, tenant, input_rows, arrived, after(down, near, *arrived), rank, 512
    )
    beside = swap(gathered, "fsdp", 1)
    pair = swap(gathered, "fsdp", 2)
    cot_x = swap(after(cotangent, *arrived, far), "dp", 2)
    partial = rank_backward(tenant, turned, after(up, gathered, for_far), lowered, 512)
    first, own = own_and_forward(
        owner[0].reshape(1), gathered, turned, after(frozen_weight, partial), 512
    )
    late = after(partial, first, cot_x)
    sums = [swap(late, "fsdp", k) for k in (1, 2, 3)]
    across = base_gradient(
        owner[2].reshape(1), turned, after(frozen_weight, first, from_near), width, 512, for_far
    )
    from_pair = swap(across, "fsdp", 2)
    diagonal = swap(after(pair, across), "fsdp", 1)
    gathered_x = swap(after(gathered, across, cot_x), "dp", 2)
    second = forward(
        jnp.stack([owner[1], owner[2]]), [beside, pair], after(frozen_weight, across), 512, first
    )
    scale = jnp.where(jnp.arange(2 * rank) < rank, 1.0, adapter_scale).astype(F32)
    ranks = ((after(partial, second, from_pair) + sums[0] + (sums[1] + sums[2])) * scale).astype(BF)
    bundle = finish_gradient([own, from_near, from_pair], tenant, ranks, after(down, second, diagonal), 512)
    bundle_x = swap(bundle, "dp", 2)
    bundle_c = swap(bundle, "dp", 1)
    cot_all = [
        cotangent,
        swap(after(cotangent, bundle), "dp", 1),
        cot_x,
        swap(after(cot_x, bundle), "dp", 1),
    ]
    outputs = forward(
        owner[3].reshape(1), [diagonal], after(frozen_weight, bundle), 512, second, tenant, ranks, up
    )
    bundles = [bundle, bundle_c, bundle_x, swap(after(bundle_x, outputs), "dp", 1)]
    grad_b = owned_gradient(
        place, slot, after(bundles, outputs), False, cot_all, share, 2 * rank, adapter_scale, 1024
    )
    row_grad = bring_home(place, handoff_counts, after(bundles, grad_b), capacity, width)
    gathered_all = [
        gathered,
        swap(after(gathered, outputs), "dp", 1),
        gathered_x,
        swap(after(gathered_x, row_grad), "dp", 1),
    ]
    grad_a = owned_gradient(
        place, slot, after(bundles, row_grad), True, gathered_all, share, 2 * rank, 1.0, 512
    )
    return (
        outputs,
        row_grad,
        grad_a.reshape(share, rank, width).transpose(0, 2, 1),
        grad_b.reshape(share, rank, hidden),
    )


def solution(mesh):
    placed = (
        P(("groups", "dp"), "fsdp"),
        P(("groups", "dp"), "fsdp"),
        P(None, "fsdp"),
        P("groups", "fsdp", None),
        P("groups", None, "fsdp"),
        P("groups", None),
        P("groups", None),
        P("groups"),
    )
    four_by_four = mesh.shape["dp"] == 4 and mesh.shape["fsdp"] == 4
    return jax.shard_map(
        fast_body if four_by_four else plain_body,
        mesh=mesh,
        in_specs=placed,
        out_specs=(
            P(("groups", "dp"), "fsdp"),
            P(("groups", "dp"), "fsdp"),
            P(("groups", "dp"), "fsdp", None),
            P(("groups", "dp"), None, "fsdp"),
        ),
        check_vma=False,
    )
```

```python
import functools

import jax
import jax.numpy as jnp
from jax import lax
from jax.experimental import pallas as pl
from jax.experimental.pallas import tpu as pltpu
from jax.sharding import PartitionSpec as P

adapter_scale = 0.25
BF = jnp.bfloat16
F32 = jnp.float32
I32 = jnp.int32
VMEM_LIMIT = 32 * 2**20


def before_sums(values, group_axis):
    return jnp.cumsum(values, axis=group_axis) - values


def find_source(starts, counts, length):
    places = jnp.arange(length, dtype=jnp.int32)[:, None]
    inside = (places >= starts[None, :]) & (places < (starts + counts)[None, :])
    numbers = jnp.arange(starts.shape[0], dtype=jnp.int32)[None, :]
    source = jnp.sum(jnp.where(inside, numbers, 0), axis=1)
    offset = places[:, 0] - jnp.sum(jnp.where(inside, starts[None, :], 0), axis=1)
    present = jnp.any(inside, axis=1)
    return (source, offset, present)


def pack_slots(values, starts, counts, width, allowed):
    places = jnp.arange(width, dtype=jnp.int32)[None, :]
    picked = jnp.minimum(starts[:, None] + places, values.shape[0] - 1)
    valid = (places < counts[:, None]) & allowed[:, None]
    taken = jnp.take(values, picked.reshape(-1), axis=0).reshape(
        counts.shape[0], width, values.shape[1]
    )
    return jnp.where(valid[:, :, None], taken, jnp.zeros((), values.dtype))


def plain_body(
    input_rows,
    cotangent,
    frozen_weight,
    adapter_down_weight,
    adapter_up_weight,
    tenant_row_counts,
    handoff_counts,
    tenant_gradient_slot,
):
    groups = lax.axis_size("dp")
    mine = lax.axis_index("dp")
    balanced_rows = cotangent.shape[0]
    capacity = input_rows.shape[0]
    feature_width = input_rows.shape[1]
    column_index = cotangent.shape[1]
    tenant_labels = adapter_up_weight.shape[0]
    group_position = adapter_up_weight.shape[1]
    sent_before = before_sums(handoff_counts, 1)
    recv_before = before_sums(handoff_counts, 0)
    my_sends = handoff_counts[mine]
    my_send_starts = sent_before[mine]
    my_recvs = handoff_counts[:, mine]
    my_recv_starts = recv_before[:, mine]
    others = jnp.arange(groups, dtype=jnp.int32) != mine
    source, offset, present = find_source(my_recv_starts, my_recvs, balanced_rows)
    source_row = sent_before[source, mine] + offset
    tenant_end = jnp.cumsum(tenant_row_counts, axis=1)
    row_tenant = jnp.sum(
        (jnp.take(tenant_end, source, axis=0) <= source_row[:, None]).astype(jnp.int32), axis=1
    )
    tenant_onehot = (
        row_tenant[:, None] == jnp.arange(tenant_labels, dtype=jnp.int32)[None, :]
    ).astype(jnp.bfloat16)
    half_slot = balanced_rows // 2
    outgoing = pack_slots(input_rows, my_send_starts, my_sends, half_slot, others)
    arrived = lax.all_to_all(outgoing, "dp", split_axis=0, concat_axis=0, tiled=True)
    pool = jnp.concatenate([arrived.reshape(groups * half_slot, feature_width), input_rows], axis=0)
    picked = jnp.where(source == mine, groups * half_slot + source_row, source * half_slot + offset)
    group_rows = jnp.take(pool, jnp.minimum(picked, pool.shape[0] - 1), axis=0)
    frozen_output = jnp.dot(
        lax.all_gather(group_rows, "fsdp", axis=1, tiled=True),
        frozen_weight,
        preferred_element_type=jnp.float32,
    )
    lowered_gathered = jnp.einsum(
        "ai,wiv->awv", group_rows, adapter_down_weight, preferred_element_type=jnp.float32
    )
    backward_gathered = jnp.einsum(
        "ku,wxu->kwx", cotangent, adapter_up_weight, preferred_element_type=jnp.float32
    )
    hot_wide = tenant_onehot.astype(jnp.float32)[:, :, None]
    down_part = jnp.sum(lowered_gathered * hot_wide, axis=1)
    back_part = jnp.sum(backward_gathered * hot_wide, axis=1)
    lowered_total, backward_total = lax.psum((down_part, back_part), "fsdp")
    adapter_input = lowered_total.astype(jnp.bfloat16)
    adapter_gradient = (adapter_scale * backward_total).astype(jnp.bfloat16)
    scattered_input = (tenant_onehot[:, :, None] * adapter_input[:, None, :]).reshape(
        balanced_rows, tenant_labels * group_position
    )
    scattered_gradient = (tenant_onehot[:, :, None] * adapter_gradient[:, None, :]).reshape(
        balanced_rows, tenant_labels * group_position
    )
    adapter_output = jnp.dot(
        scattered_input,
        adapter_up_weight.reshape(tenant_labels * group_position, column_index),
        preferred_element_type=jnp.float32,
    )
    adapter_backward = lax.dot_general(
        scattered_gradient,
        adapter_down_weight.transpose(1, 0, 2).reshape(
            feature_width, tenant_labels * group_position
        ),
        (((1,), (1,)), ((), ())),
        preferred_element_type=jnp.float32,
    )
    outputs = (frozen_output + adapter_scale * adapter_output).astype(jnp.bfloat16)
    grad_terms = lax.dot_general(
        cotangent, frozen_weight, (((1,), (1,)), ((), ())), preferred_element_type=jnp.float32
    )
    frozen_gradient = lax.psum_scatter(grad_terms, "fsdp", scatter_dimension=1, tiled=True)
    group_gradient = (frozen_gradient + adapter_backward).astype(jnp.bfloat16)
    part_a = lax.dot_general(
        group_rows, scattered_gradient, (((0,), (0,)), ((), ())), preferred_element_type=jnp.float32
    )
    part_a = part_a.reshape(feature_width, tenant_labels, group_position).transpose(1, 0, 2)
    partial_up = adapter_scale * lax.dot_general(
        scattered_input, cotangent, (((0,), (0,)), ((), ())), preferred_element_type=jnp.float32
    )
    partial_up = partial_up.reshape(tenant_labels, group_position, column_index)
    order = jnp.argsort(tenant_gradient_slot)
    share = tenant_labels // groups
    owner_a = (
        jnp.take(part_a, order, axis=0)
        .astype(jnp.bfloat16)
        .reshape(groups, share, feature_width, group_position)
    )
    owner_b = (
        jnp.take(partial_up, order, axis=0)
        .astype(jnp.bfloat16)
        .reshape(groups, share, group_position, column_index)
    )
    source_home, offset_home, present_home = find_source(my_send_starts, my_sends, capacity)
    half_slot = balanced_rows // 2
    back_slots = pack_slots(group_gradient, my_recv_starts, my_recvs, half_slot, others)
    home, sums_a, sums_b = (
        lax.all_to_all(back_slots, "dp", split_axis=0, concat_axis=0, tiled=True),
        lax.all_to_all(owner_a, "dp", split_axis=0, concat_axis=0, tiled=True),
        lax.all_to_all(owner_b, "dp", split_axis=0, concat_axis=0, tiled=True),
    )
    pool_home = jnp.concatenate(
        [home.reshape(groups * half_slot, feature_width), group_gradient], axis=0
    )
    picked_home = jnp.where(
        source_home == mine,
        groups * half_slot + recv_before[mine, mine] + offset_home,
        source_home * half_slot + offset_home,
    )
    row_grad = jnp.take(pool_home, jnp.minimum(picked_home, pool_home.shape[0] - 1), axis=0)
    row_grad = jnp.where(present_home[:, None], row_grad, jnp.zeros((), jnp.bfloat16))
    grad_a = jnp.sum(sums_a.astype(jnp.float32), axis=0).astype(jnp.bfloat16)
    grad_b = jnp.sum(sums_b.astype(jnp.float32), axis=0).astype(jnp.bfloat16)
    return (outputs, row_grad, grad_a, grad_b)


def params(limit=VMEM_LIMIT):
    return pltpu.CompilerParams(vmem_limit_bytes=limit)


def cost(flops, moved):
    return pl.CostEstimate(flops=int(flops) // 1000, bytes_accessed=int(moved) // 1000, transcendentals=0)


SMEM = functools.partial(pl.BlockSpec, memory_space=pltpu.SMEM)


def whole(shape):
    return pl.BlockSpec(shape, lambda *_: (0,) * len(shape))


def before(handoff_ref, giver, taker, groups):
    sent = jnp.int32(0)
    got = jnp.int32(0)
    for other in range(groups):
        sent = sent + jnp.where(other < taker, handoff_ref[giver, other], 0)
        got = got + jnp.where(other < giver, handoff_ref[other, taker], 0)
    return sent, got


def pack(place, handoff, counts, slots, rows, balanced, half):
    groups, tenants = counts.shape
    capacity, width = rows.shape

    def kernel(place_ref, handoff_ref, slots_ref, counts_ref, rows_ref, *outs):
        out_refs, tenant_ref, slot_ref = outs[: groups - 1], outs[groups - 1], outs[groups]
        mine = place_ref[0]
        here = lax.broadcasted_iota(I32, (half, capacity), 1)
        slot = lax.broadcasted_iota(I32, (half, capacity), 0)
        for step in range(1, groups):
            partner = mine ^ step
            sent, _ = before(handoff_ref, mine, partner, groups)
            pick = (here == slot + sent) & (slot < handoff_ref[mine, partner])
            out_refs[step - 1][...] = jnp.dot(
                pick.astype(F32).astype(BF), rows_ref[...], preferred_element_type=F32
            ).astype(BF)
        upto = lax.broadcasted_iota(I32, (tenants, tenants), 1) <= lax.broadcasted_iota(
            I32, (tenants, tenants), 0
        )
        ends = lax.dot_general(
            upto.astype(F32).astype(BF),
            counts_ref[...].astype(F32).astype(BF),
            (((1,), (1,)), ((), ())),
            preferred_element_type=F32,
        ).astype(I32)
        place_of = lax.broadcasted_iota(I32, (1, balanced), 1)
        for step in range(groups):
            taker = mine ^ step
            position = place_of
            row_ends = jnp.zeros((tenants, balanced), I32)
            for giver in range(groups):
                sent, got = before(handoff_ref, giver, taker, groups)
                inside = (place_of >= got) & (place_of < got + handoff_ref[giver, taker])
                position = position + jnp.where(inside, sent - got, 0)
                row_ends = row_ends + jnp.where(inside, ends[:, giver : giver + 1], 0)
            tenant = jnp.sum((row_ends <= position).astype(I32), axis=0, keepdims=True)
            target = jnp.zeros((1, balanced), I32)
            for label in range(tenants):
                target = target + jnp.where(tenant == label, slots_ref[label], 0)
            tenant_ref[step : step + 1, :] = tenant
            slot_ref[step : step + 1, :] = target

    return pl.pallas_call(
        kernel,
        in_specs=[SMEM(), SMEM(), SMEM(), pl.BlockSpec(memory_space=pltpu.VMEM), pl.BlockSpec(memory_space=pltpu.VMEM)],
        out_shape=[jax.ShapeDtypeStruct((half, width), BF)] * (groups - 1)
        + [jax.ShapeDtypeStruct((groups, balanced), I32)] * 2,
        compiler_params=params(60 * 2**20),
        cost_estimate=cost(2 * 3 * half * capacity * width, 2 * capacity * width * 2),
    )(place, handoff, slots, counts, rows)


def masked_rank(product, tenant, first, rank):
    total = jnp.zeros((rank, product.shape[1]), F32)
    for label in range(product.shape[0] // rank):
        total = total + jnp.where(tenant == first + label, product[label * rank : (label + 1) * rank], 0.0)
    return total


def unpack(place, handoff, tenant, rows, arrived, down, rank, block):
    groups, balanced = tenant.shape
    capacity, width = rows.shape
    half = arrived[0].shape[0]

    def kernel(place_ref, handoff_ref, tenant_ref, rows_ref, *refs):
        arrived_refs = refs[: groups - 1]
        down_ref, gathered_ref, lowered_ref, turned = refs[groups - 1 :]
        step = pl.program_id(0)

        @pl.when(step == 0)
        def _():
            mine = place_ref[0]
            place_of = lax.broadcasted_iota(I32, (balanced, capacity), 0)
            here = lax.broadcasted_iota(I32, (balanced, capacity), 1)
            sent, got = before(handoff_ref, mine, mine, groups)
            inside = (place_of >= got) & (place_of < got + handoff_ref[mine, mine])
            pick = inside & (here == place_of - got + sent)
            total = jnp.dot(pick.astype(F32).astype(BF), rows_ref[...], preferred_element_type=F32)
            place_of = lax.broadcasted_iota(I32, (balanced, half), 0)
            here = lax.broadcasted_iota(I32, (balanced, half), 1)
            for k in range(1, groups):
                giver = mine ^ k
                _, got = before(handoff_ref, giver, mine, groups)
                inside = (place_of >= got) & (place_of < got + handoff_ref[giver, mine])
                pick = inside & (here == place_of - got)
                total = total + jnp.dot(
                    pick.astype(F32).astype(BF), arrived_refs[k - 1][...], preferred_element_type=F32
                )
            gathered_ref[...] = total.astype(BF)
            turned[...] = total.T.astype(BF)
            lowered_ref[...] = jnp.zeros_like(lowered_ref)

        product = jnp.dot(down_ref[...], turned[...], preferred_element_type=F32)
        lowered_ref[...] += masked_rank(product, tenant_ref[0:1, :], step * (block // rank), rank)

    return pl.pallas_call(
        kernel,
        grid=(down.shape[0] // block,),
        in_specs=[SMEM(), SMEM(), whole((groups, balanced)), whole((capacity, width))]
        + [whole((half, width))] * (groups - 1)
        + [pl.BlockSpec((block, width), lambda i: (i, 0))],
        out_specs=[whole((balanced, width)), whole((rank, balanced))],
        out_shape=[
            jax.ShapeDtypeStruct((balanced, width), BF),
            jax.ShapeDtypeStruct((rank, balanced), F32),
        ],
        scratch_shapes=[pltpu.VMEM((width, balanced), BF)],
        compiler_params=params(),
        cost_estimate=cost(2 * balanced * down.size, 2 * down.size + 6 * balanced * width),
    )(place, handoff, tenant, rows, *arrived, down)


def rank_backward(tenant, turned, up, lowered, block):
    rank, balanced = lowered.shape
    hidden = up.shape[1]
    steps = up.shape[0] // block

    def kernel(tenant_ref, turned_ref, lowered_ref, up_ref, out_ref, total_ref):
        step = pl.program_id(0)

        @pl.when(step == 0)
        def _():
            total_ref[:rank, :] = lowered_ref[...]
            total_ref[rank:, :] = jnp.zeros((rank, balanced), F32)

        product = jnp.dot(up_ref[...], turned_ref[...], preferred_element_type=F32)
        total_ref[rank:, :] += masked_rank(product, tenant_ref[0:1, :], step * (block // rank), rank)

        @pl.when(step == steps - 1)
        def _():
            out_ref[...] = total_ref[...].T

    return pl.pallas_call(
        kernel,
        grid=(steps,),
        in_specs=[
            whole(tenant.shape), whole(turned.shape), whole(lowered.shape),
            pl.BlockSpec((block, hidden), lambda i: (i, 0)),
        ],
        out_specs=whole((balanced, 2 * rank)),
        out_shape=jax.ShapeDtypeStruct((balanced, 2 * rank), F32),
        scratch_shapes=[pltpu.VMEM((2 * rank, balanced), F32)],
        compiler_params=params(50 * 2**20),
        cost_estimate=cost(2 * balanced * up.size, 2 * up.size),
    )(tenant, turned, lowered, up)


def base_gradient(owner, turned, weight, width, block, arrived=None):
    hidden, balanced = turned.shape
    steps = width // block

    def kernel(owner_ref, turned_ref, weight_ref, *refs):
        product = jnp.dot(weight_ref[...], turned_ref[...], preferred_element_type=F32).T
        if arrived is not None:
            product = product + refs[0][...].astype(F32)
        refs[-1][...] = product.astype(BF)

    piece = pl.BlockSpec((balanced, block), lambda i, owner_ref: (0, i))
    return pl.pallas_call(
        kernel,
        grid_spec=pltpu.PrefetchScalarGridSpec(
            num_scalar_prefetch=1,
            grid=(steps,),
            in_specs=[
                whole(turned.shape),
                pl.BlockSpec((block, hidden), lambda i, owner_ref: (owner_ref[0] * steps + i, 0)),
            ]
            + ([] if arrived is None else [piece]),
            out_specs=piece,
        ),
        out_shape=jax.ShapeDtypeStruct((balanced, width), BF),
        compiler_params=params(),
        cost_estimate=cost(2 * balanced * width * hidden, 2 * width * hidden),
    )(owner, turned, weight, *(() if arrived is None else (arrived,)))


def turn_and_far(owner, cotangent, weight, width, block):
    balanced, hidden = cotangent.shape
    steps = width // block

    def kernel(owner_ref, cotangent_ref, weight_ref, far_ref, turned_ref):
        @pl.when(pl.program_id(0) == 0)
        def _():
            turned_ref[...] = cotangent_ref[...].astype(F32).T.astype(BF)

        far_ref[...] = jnp.dot(weight_ref[...], turned_ref[...], preferred_element_type=F32).T.astype(BF)

    return pl.pallas_call(
        kernel,
        grid_spec=pltpu.PrefetchScalarGridSpec(
            num_scalar_prefetch=1,
            grid=(steps,),
            in_specs=[
                whole(cotangent.shape),
                pl.BlockSpec((block, hidden), lambda i, o: (o[0] * steps + i, 0)),
            ],
            out_specs=[pl.BlockSpec((balanced, block), lambda i, o: (0, i)), whole((hidden, balanced))],
        ),
        out_shape=[
            jax.ShapeDtypeStruct((balanced, width), BF),
            jax.ShapeDtypeStruct((hidden, balanced), BF),
        ],
        compiler_params=params(),
        cost_estimate=cost(2 * balanced * width * hidden, 2 * width * hidden),
    )(owner, cotangent, weight)


def spread(wide_ref, tenant_ref, ranks_ref, second, scale, tenants, rank):
    balanced, lanes = ranks_ref.shape
    vectors = scale * ranks_ref[...].astype(F32)
    turned = pltpu.roll(vectors, rank, 1)
    high = lax.broadcasted_iota(I32, (balanced, lanes), 1) >= rank
    twice = jnp.where(high, vectors, turned) if second else jnp.where(high, turned, vectors)
    half = (lax.broadcasted_iota(I32, (lanes, balanced), 0) >= rank).astype(F32)
    label = (tenant_ref[0:1, :].astype(F32) - half).T
    for pair in range(tenants // 2):
        wide_ref[:, pair * lanes : (pair + 1) * lanes] = jnp.where(label == 2.0 * pair, twice, 0.0).astype(BF)


def own_and_forward(owner, part, turned, weight, block):
    balanced, width = part.shape
    hidden = weight.shape[1]
    steps = width // block

    def kernel(owner_ref, part_ref, turned_ref, weight_ref, total_ref, own_ref):
        own_ref[...] = jnp.dot(weight_ref[...], turned_ref[...], preferred_element_type=F32).T.astype(BF)
        piece = jnp.dot(part_ref[...], weight_ref[...], preferred_element_type=F32)

        @pl.when(pl.program_id(0) == 0)
        def _():
            total_ref[...] = piece

        @pl.when(pl.program_id(0) > 0)
        def _():
            total_ref[...] += piece

    columns = pl.BlockSpec((balanced, block), lambda i, o: (0, i))
    return pl.pallas_call(
        kernel,
        grid_spec=pltpu.PrefetchScalarGridSpec(
            num_scalar_prefetch=1,
            grid=(steps,),
            in_specs=[
                columns,
                whole(turned.shape),
                pl.BlockSpec((block, hidden), lambda i, o: (o[0] * steps + i, 0)),
            ],
            out_specs=[whole((balanced, hidden)), columns],
        ),
        out_shape=[
            jax.ShapeDtypeStruct((balanced, hidden), F32),
            jax.ShapeDtypeStruct((balanced, width), BF),
        ],
        compiler_params=params(),
        cost_estimate=cost(4 * balanced * width * hidden, 2 * width * hidden),
    )(owner, part, turned, weight)


def forward(owners, parts, weight, block, total=None, tenant=None, ranks=None, up=None):
    balanced, width = parts[0].shape
    hidden = weight.shape[1]
    count = len(parts)
    last = up is not None

    def kernel(owners_ref, *refs):
        part_refs, weight_refs = refs[:count], refs[count : 2 * count]
        rest = list(refs[2 * count :])
        value = jnp.dot(part_refs[0][...], weight_refs[0][...], preferred_element_type=F32)
        for i in range(1, count):
            value = value + jnp.dot(part_refs[i][...], weight_refs[i][...], preferred_element_type=F32)
        if total is not None:
            value = value + rest.pop(0)[...]
        if last:
            tenant_ref, ranks_ref, up_ref = rest.pop(0), rest.pop(0), rest.pop(0)
            wide_ref = rest.pop()

            @pl.when(pl.program_id(0) == 0)
            def _():
                rank = ranks.shape[1] // 2
                spread(wide_ref, tenant_ref, ranks_ref, False, adapter_scale, up.shape[0] // rank, rank)

            value = value + jnp.dot(wide_ref[...], up_ref[...], preferred_element_type=F32)
        rest[0][...] = value.astype(rest[0].dtype)

    piece = pl.BlockSpec((balanced, block), lambda i, o: (0, i))
    in_specs = [whole((balanced, width))] * count
    for i in range(count):
        in_specs.append(pl.BlockSpec((width, block), lambda n, o, i=i: (o[i], n)))
    operands = [*parts, *([weight] * count)]
    if total is not None:
        in_specs.append(piece)
        operands.append(total)
    if last:
        in_specs += [whole(tenant.shape), whole(ranks.shape), pl.BlockSpec((up.shape[0], block), lambda i, o: (0, i))]
        operands += [tenant, ranks, up]
    return pl.pallas_call(
        kernel,
        grid_spec=pltpu.PrefetchScalarGridSpec(
            num_scalar_prefetch=1,
            grid=(hidden // block,),
            in_specs=in_specs,
            out_specs=piece,
            scratch_shapes=[pltpu.VMEM((balanced, up.shape[0]), BF)] if last else [],
        ),
        out_shape=jax.ShapeDtypeStruct((balanced, hidden), BF if last else F32),
        compiler_params=params(50 * 2**20 if last else VMEM_LIMIT),
        cost_estimate=cost(
            2 * balanced * hidden * (count * width + (up.shape[0] if last else 0)),
            2 * hidden * (count * width + (up.shape[0] if last else 0)),
        ),
    )(owners, *operands)


def finish_gradient(terms, tenant, ranks, down, block):
    balanced, width = terms[0].shape

    lanes = ranks.shape[1]
    rank = lanes // 2

    def kernel(tenant_ref, ranks_ref, down_ref, *refs):
        term_refs, out_ref, wide_ref = refs[:-2], refs[-2], refs[-1]
        spread(wide_ref, tenant_ref, ranks_ref, True, 1.0, down.shape[0] // rank, rank)
        for start in range(0, width, block):
            at = pl.ds(start, block)
            value = jnp.dot(wide_ref[...], down_ref[:, at], preferred_element_type=F32)
            for term_ref in term_refs:
                value = value + term_ref[:, at].astype(F32)
            out_ref[:, at] = value.astype(BF)
        out_ref[:, pl.ds(width, lanes)] = ranks_ref[...]

    return pl.pallas_call(
        kernel,
        grid=(1,),
        in_specs=[whole(tenant.shape), whole(ranks.shape), whole(down.shape)] + [whole((balanced, width))] * len(terms),
        out_specs=whole((balanced, width + lanes)),
        out_shape=jax.ShapeDtypeStruct((balanced, width + lanes), BF),
        scratch_shapes=[pltpu.VMEM((balanced, down.shape[0]), BF)],
        compiler_params=params(),
        cost_estimate=cost(2 * balanced * down.size, 2 * down.size),
    )(tenant, ranks, down, *terms)


def owned_gradient(place, slot, bundles, second, values, share, lanes, scale, block):
    groups, balanced = slot.shape
    rank = lanes // 2
    width = values[0].shape[1]
    column = bundles[0].shape[1] // lanes - 1

    def kernel(place_ref, slot_ref, *refs):
        rank_refs, value_refs = refs[:groups], refs[groups : 2 * groups]
        out_ref, wide_ref = refs[2 * groups :]

        @pl.when(pl.program_id(0) == 0)
        def _():
            first = place_ref[0] * share
            for k in range(groups):
                turned = rank_refs[k][...].astype(F32).T
                mine = turned[rank:, :] if second else turned[:rank, :]
                for s in range(share):
                    wide_ref[k, s * rank : (s + 1) * rank, :] = jnp.where(
                        slot_ref[k : k + 1, :] == first + s, mine, 0.0
                    ).astype(BF)

        value = jnp.dot(wide_ref[0], value_refs[0][...], preferred_element_type=F32)
        for k in range(1, groups):
            value = value + jnp.dot(wide_ref[k], value_refs[k][...], preferred_element_type=F32)
        out_ref[...] = (scale * value).astype(BF)

    return pl.pallas_call(
        kernel,
        grid=(width // block,),
        in_specs=[SMEM(), whole(slot.shape)]
        + [pl.BlockSpec((balanced, lanes), lambda i: (0, column))] * groups
        + [pl.BlockSpec((balanced, block), lambda i: (0, i))] * groups,
        out_specs=pl.BlockSpec((share * rank, block), lambda i: (0, i)),
        out_shape=jax.ShapeDtypeStruct((share * rank, width), BF),
        scratch_shapes=[pltpu.VMEM((groups, share * rank, balanced), BF)],
        compiler_params=params(),
        cost_estimate=cost(2 * groups * balanced * share * rank * width, 2 * width * (groups * balanced + share * rank)),
    )(place, slot, *bundles, *values)


def bring_home(place, handoff, bundles, capacity, width):
    balanced = bundles[0].shape[0]
    groups = handoff.shape[0]

    def kernel(place_ref, handoff_ref, *refs):
        out_ref = refs[-1]
        mine = place_ref[0]
        row = lax.broadcasted_iota(I32, (capacity, balanced), 0)
        here = lax.broadcasted_iota(I32, (capacity, balanced), 1)
        total = jnp.zeros((capacity, width), F32)
        for k in range(groups):
            taker = mine ^ k
            sent, got = before(handoff_ref, mine, taker, groups)
            inside = (row >= sent) & (row < sent + handoff_ref[mine, taker])
            pick = inside & (here == row - sent + got)
            total = total + jnp.dot(pick.astype(F32).astype(BF), refs[k][...], preferred_element_type=F32)
        out_ref[...] = total.astype(BF)

    return pl.pallas_call(
        kernel,
        grid=(1,),
        in_specs=[SMEM(), SMEM()] + [whole((balanced, width))] * groups,
        out_specs=whole((capacity, width)),
        out_shape=jax.ShapeDtypeStruct((capacity, width), BF),
        compiler_params=params(),
        cost_estimate=cost(2 * groups * balanced * capacity * width, 4 * groups * balanced * width),
    )(place, handoff, *bundles)


def swap(values, axis, distance):
    size = lax.axis_size(axis)
    return lax.ppermute(values, axis, [(i, i ^ distance) for i in range(size)])


def after(values, *earlier):
    return lax.optimization_barrier((values, *earlier))[0]


def fast_body(
    input_rows,
    cotangent,
    frozen_weight,
    adapter_down_weight,
    adapter_up_weight,
    tenant_row_counts,
    handoff_counts,
    tenant_gradient_slot,
):
    mine = lax.axis_index("dp")
    z = lax.axis_index("fsdp")
    balanced = cotangent.shape[0]
    capacity, width = input_rows.shape
    tenants, rank, hidden = adapter_up_weight.shape
    share = tenants // lax.axis_size("dp")
    place = mine.astype(I32).reshape(1)
    owner = [(z ^ k).astype(I32) for k in range(4)]
    down = adapter_down_weight.transpose(0, 2, 1).reshape(tenants * rank, width)
    up = adapter_up_weight.reshape(tenants * rank, hidden)

    *outgoing, tenant, slot = pack(
        place, handoff_counts, tenant_row_counts, tenant_gradient_slot, input_rows, balanced, balanced // 2
    )
    arrived = [None] * 3
    for k in (2, 3, 1):
        arrived[k - 1] = swap(outgoing[k - 1], "dp", k)
    far, turned = turn_and_far(
        owner[3].reshape(1), cotangent, after(frozen_weight, tenant), width, 512
    )
    for_far = swap(far, "fsdp", 1)
    near = base_gradient(owner[1].reshape(1), turned, after(frozen_weight, far), width, 512)
    from_near = swap(near, "fsdp", 1)
    gathered, lowered = unpack(
        place, handoff_counts, tenant, input_rows, arrived, after(down, near, *arrived), rank, 512
    )
    beside = swap(gathered, "fsdp", 1)
    pair = swap(gathered, "fsdp", 2)
    cot_x = swap(after(cotangent, *arrived, far), "dp", 2)
    across = base_gradient(owner[2].reshape(1), turned, after(frozen_weight, gathered), width, 512, for_far)
    from_pair = swap(across, "fsdp", 2)
    partial = rank_backward(tenant, turned, after(up, across), lowered, 512)
    first, own = own_and_forward(
        owner[0].reshape(1), gathered, turned, after(frozen_weight, partial, from_near), 512
    )
    late = after(partial, first, cot_x, beside)
    sums = [swap(late, "fsdp", k) for k in (1, 2, 3)]
    diagonal = swap(after(pair, first), "fsdp", 1)
    gathered_x = swap(after(gathered, first, cot_x), "dp", 2)
    second = forward(
        jnp.stack([owner[1], owner[2]]), [beside, pair], after(frozen_weight, first), 512, first
    )
    scale = jnp.where(jnp.arange(2 * rank) < rank, 1.0, adapter_scale).astype(F32)
    ranks = ((after(partial, second, from_pair) + sums[0] + (sums[1] + sums[2])) * scale).astype(BF)
    bundle = finish_gradient([own, from_near, from_pair], tenant, ranks, after(down, second, diagonal), 512)
    bundle_x = swap(bundle, "dp", 2)
    bundle_c = swap(bundle, "dp", 1)
    cot_all = [
        cotangent,
        swap(after(cotangent, bundle), "dp", 1),
        cot_x,
        swap(after(cot_x, bundle), "dp", 1),
    ]
    outputs = forward(
        owner[3].reshape(1), [diagonal], after(frozen_weight, bundle), 512, second, tenant, ranks, up
    )
    bundles = [bundle, bundle_c, bundle_x, swap(after(bundle_x, outputs), "dp", 1)]
    grad_b = owned_gradient(
        place, slot, after(bundles, outputs), False, cot_all, share, 2 * rank, adapter_scale, 1024
    )
    row_grad = bring_home(place, handoff_counts, after(bundles, grad_b), capacity, width)
    gathered_all = [
        gathered,
        swap(after(gathered, outputs), "dp", 1),
        gathered_x,
        swap(after(gathered_x, row_grad), "dp", 1),
    ]
    grad_a = owned_gradient(
        place, slot, after(bundles, row_grad), True, gathered_all, share, 2 * rank, 1.0, 512
    )
    return (
        outputs,
        row_grad,
        grad_a.reshape(share, rank, width).transpose(0, 2, 1),
        grad_b.reshape(share, rank, hidden),
    )


def solution(mesh):
    placed = (
        P(("groups", "dp"), "fsdp"),
        P(("groups", "dp"), "fsdp"),
        P(None, "fsdp"),
        P("groups", "fsdp", None),
        P("groups", None, "fsdp"),
        P("groups", None),
        P("groups", None),
        P("groups"),
    )
    four_by_four = mesh.shape["dp"] == 4 and mesh.shape["fsdp"] == 4
    return jax.shard_map(
        fast_body if four_by_four else plain_body,
        mesh=mesh,
        in_specs=placed,
        out_specs=(
            P(("groups", "dp"), "fsdp"),
            P(("groups", "dp"), "fsdp"),
            P(("groups", "dp"), "fsdp", None),
            P(("groups", "dp"), None, "fsdp"),
        ),
        check_vma=False,
    )
```

```python
import functools

import jax
import jax.numpy as jnp
from jax import lax
from jax.experimental import pallas as pl
from jax.experimental.pallas import tpu as pltpu
from jax.sharding import PartitionSpec as P

adapter_scale = 0.25
BF = jnp.bfloat16
F32 = jnp.float32
I32 = jnp.int32
VMEM_LIMIT = 32 * 2**20


def before_sums(values, group_axis):
    return jnp.cumsum(values, axis=group_axis) - values


def find_source(starts, counts, length):
    places = jnp.arange(length, dtype=jnp.int32)[:, None]
    inside = (places >= starts[None, :]) & (places < (starts + counts)[None, :])
    numbers = jnp.arange(starts.shape[0], dtype=jnp.int32)[None, :]
    source = jnp.sum(jnp.where(inside, numbers, 0), axis=1)
    offset = places[:, 0] - jnp.sum(jnp.where(inside, starts[None, :], 0), axis=1)
    present = jnp.any(inside, axis=1)
    return (source, offset, present)


def pack_slots(values, starts, counts, width, allowed):
    places = jnp.arange(width, dtype=jnp.int32)[None, :]
    picked = jnp.minimum(starts[:, None] + places, values.shape[0] - 1)
    valid = (places < counts[:, None]) & allowed[:, None]
    taken = jnp.take(values, picked.reshape(-1), axis=0).reshape(
        counts.shape[0], width, values.shape[1]
    )
    return jnp.where(valid[:, :, None], taken, jnp.zeros((), values.dtype))


def plain_body(
    input_rows,
    cotangent,
    frozen_weight,
    adapter_down_weight,
    adapter_up_weight,
    tenant_row_counts,
    handoff_counts,
    tenant_gradient_slot,
):
    groups = lax.axis_size("dp")
    mine = lax.axis_index("dp")
    balanced_rows = cotangent.shape[0]
    capacity = input_rows.shape[0]
    feature_width = input_rows.shape[1]
    column_index = cotangent.shape[1]
    tenant_labels = adapter_up_weight.shape[0]
    group_position = adapter_up_weight.shape[1]
    sent_before = before_sums(handoff_counts, 1)
    recv_before = before_sums(handoff_counts, 0)
    my_sends = handoff_counts[mine]
    my_send_starts = sent_before[mine]
    my_recvs = handoff_counts[:, mine]
    my_recv_starts = recv_before[:, mine]
    others = jnp.arange(groups, dtype=jnp.int32) != mine
    source, offset, present = find_source(my_recv_starts, my_recvs, balanced_rows)
    source_row = sent_before[source, mine] + offset
    tenant_end = jnp.cumsum(tenant_row_counts, axis=1)
    row_tenant = jnp.sum(
        (jnp.take(tenant_end, source, axis=0) <= source_row[:, None]).astype(jnp.int32), axis=1
    )
    tenant_onehot = (
        row_tenant[:, None] == jnp.arange(tenant_labels, dtype=jnp.int32)[None, :]
    ).astype(jnp.bfloat16)
    half_slot = balanced_rows // 2
    outgoing = pack_slots(input_rows, my_send_starts, my_sends, half_slot, others)
    arrived = lax.all_to_all(outgoing, "dp", split_axis=0, concat_axis=0, tiled=True)
    pool = jnp.concatenate([arrived.reshape(groups * half_slot, feature_width), input_rows], axis=0)
    picked = jnp.where(source == mine, groups * half_slot + source_row, source * half_slot + offset)
    group_rows = jnp.take(pool, jnp.minimum(picked, pool.shape[0] - 1), axis=0)
    frozen_output = jnp.dot(
        lax.all_gather(group_rows, "fsdp", axis=1, tiled=True),
        frozen_weight,
        preferred_element_type=jnp.float32,
    )
    lowered_gathered = jnp.einsum(
        "ai,wiv->awv", group_rows, adapter_down_weight, preferred_element_type=jnp.float32
    )
    backward_gathered = jnp.einsum(
        "ku,wxu->kwx", cotangent, adapter_up_weight, preferred_element_type=jnp.float32
    )
    hot_wide = tenant_onehot.astype(jnp.float32)[:, :, None]
    down_part = jnp.sum(lowered_gathered * hot_wide, axis=1)
    back_part = jnp.sum(backward_gathered * hot_wide, axis=1)
    lowered_total, backward_total = lax.psum((down_part, back_part), "fsdp")
    adapter_input = lowered_total.astype(jnp.bfloat16)
    adapter_gradient = (adapter_scale * backward_total).astype(jnp.bfloat16)
    scattered_input = (tenant_onehot[:, :, None] * adapter_input[:, None, :]).reshape(
        balanced_rows, tenant_labels * group_position
    )
    scattered_gradient = (tenant_onehot[:, :, None] * adapter_gradient[:, None, :]).reshape(
        balanced_rows, tenant_labels * group_position
    )
    adapter_output = jnp.dot(
        scattered_input,
        adapter_up_weight.reshape(tenant_labels * group_position, column_index),
        preferred_element_type=jnp.float32,
    )
    adapter_backward = lax.dot_general(
        scattered_gradient,
        adapter_down_weight.transpose(1, 0, 2).reshape(
            feature_width, tenant_labels * group_position
        ),
        (((1,), (1,)), ((), ())),
        preferred_element_type=jnp.float32,
    )
    outputs = (frozen_output + adapter_scale * adapter_output).astype(jnp.bfloat16)
    grad_terms = lax.dot_general(
        cotangent, frozen_weight, (((1,), (1,)), ((), ())), preferred_element_type=jnp.float32
    )
    frozen_gradient = lax.psum_scatter(grad_terms, "fsdp", scatter_dimension=1, tiled=True)
    group_gradient = (frozen_gradient + adapter_backward).astype(jnp.bfloat16)
    part_a = lax.dot_general(
        group_rows, scattered_gradient, (((0,), (0,)), ((), ())), preferred_element_type=jnp.float32
    )
    part_a = part_a.reshape(feature_width, tenant_labels, group_position).transpose(1, 0, 2)
    partial_up = adapter_scale * lax.dot_general(
        scattered_input, cotangent, (((0,), (0,)), ((), ())), preferred_element_type=jnp.float32
    )
    partial_up = partial_up.reshape(tenant_labels, group_position, column_index)
    order = jnp.argsort(tenant_gradient_slot)
    share = tenant_labels // groups
    owner_a = (
        jnp.take(part_a, order, axis=0)
        .astype(jnp.bfloat16)
        .reshape(groups, share, feature_width, group_position)
    )
    owner_b = (
        jnp.take(partial_up, order, axis=0)
        .astype(jnp.bfloat16)
        .reshape(groups, share, group_position, column_index)
    )
    source_home, offset_home, present_home = find_source(my_send_starts, my_sends, capacity)
    half_slot = balanced_rows // 2
    back_slots = pack_slots(group_gradient, my_recv_starts, my_recvs, half_slot, others)
    home, sums_a, sums_b = (
        lax.all_to_all(back_slots, "dp", split_axis=0, concat_axis=0, tiled=True),
        lax.all_to_all(owner_a, "dp", split_axis=0, concat_axis=0, tiled=True),
        lax.all_to_all(owner_b, "dp", split_axis=0, concat_axis=0, tiled=True),
    )
    pool_home = jnp.concatenate(
        [home.reshape(groups * half_slot, feature_width), group_gradient], axis=0
    )
    picked_home = jnp.where(
        source_home == mine,
        groups * half_slot + recv_before[mine, mine] + offset_home,
        source_home * half_slot + offset_home,
    )
    row_grad = jnp.take(pool_home, jnp.minimum(picked_home, pool_home.shape[0] - 1), axis=0)
    row_grad = jnp.where(present_home[:, None], row_grad, jnp.zeros((), jnp.bfloat16))
    grad_a = jnp.sum(sums_a.astype(jnp.float32), axis=0).astype(jnp.bfloat16)
    grad_b = jnp.sum(sums_b.astype(jnp.float32), axis=0).astype(jnp.bfloat16)
    return (outputs, row_grad, grad_a, grad_b)


def params(limit=VMEM_LIMIT):
    return pltpu.CompilerParams(vmem_limit_bytes=limit)


def cost(flops, moved):
    return pl.CostEstimate(flops=int(flops) // 1000, bytes_accessed=int(moved) // 1000, transcendentals=0)


SMEM = functools.partial(pl.BlockSpec, memory_space=pltpu.SMEM)


def whole(shape):
    return pl.BlockSpec(shape, lambda *_: (0,) * len(shape))


def before(handoff_ref, giver, taker, groups):
    sent = jnp.int32(0)
    got = jnp.int32(0)
    for other in range(groups):
        sent = sent + jnp.where(other < taker, handoff_ref[giver, other], 0)
        got = got + jnp.where(other < giver, handoff_ref[other, taker], 0)
    return sent, got


def pack(place, handoff, counts, slots, rows, balanced, half):
    groups, tenants = counts.shape
    capacity, width = rows.shape

    def kernel(place_ref, handoff_ref, slots_ref, counts_ref, rows_ref, *outs):
        out_refs, tenant_ref, slot_ref = outs[: groups - 1], outs[groups - 1], outs[groups]
        mine = place_ref[0]
        here = lax.broadcasted_iota(I32, (half, capacity), 1)
        slot = lax.broadcasted_iota(I32, (half, capacity), 0)
        for step in range(1, groups):
            partner = mine ^ step
            sent, _ = before(handoff_ref, mine, partner, groups)
            pick = (here == slot + sent) & (slot < handoff_ref[mine, partner])
            out_refs[step - 1][...] = jnp.dot(
                pick.astype(F32).astype(BF), rows_ref[...], preferred_element_type=F32
            ).astype(BF)
        upto = lax.broadcasted_iota(I32, (tenants, tenants), 1) <= lax.broadcasted_iota(
            I32, (tenants, tenants), 0
        )
        ends = lax.dot_general(
            upto.astype(F32).astype(BF),
            counts_ref[...].astype(F32).astype(BF),
            (((1,), (1,)), ((), ())),
            preferred_element_type=F32,
        ).astype(I32)
        place_of = lax.broadcasted_iota(I32, (1, balanced), 1)
        for step in range(groups):
            taker = mine ^ step
            position = place_of
            row_ends = jnp.zeros((tenants, balanced), I32)
            for giver in range(groups):
                sent, got = before(handoff_ref, giver, taker, groups)
                inside = (place_of >= got) & (place_of < got + handoff_ref[giver, taker])
                position = position + jnp.where(inside, sent - got, 0)
                row_ends = row_ends + jnp.where(inside, ends[:, giver : giver + 1], 0)
            tenant = jnp.sum((row_ends <= position).astype(I32), axis=0, keepdims=True)
            target = jnp.zeros((1, balanced), I32)
            for label in range(tenants):
                target = target + jnp.where(tenant == label, slots_ref[label], 0)
            tenant_ref[step : step + 1, :] = tenant
            slot_ref[step : step + 1, :] = target

    return pl.pallas_call(
        kernel,
        in_specs=[SMEM(), SMEM(), SMEM(), pl.BlockSpec(memory_space=pltpu.VMEM), pl.BlockSpec(memory_space=pltpu.VMEM)],
        out_shape=[jax.ShapeDtypeStruct((half, width), BF)] * (groups - 1)
        + [jax.ShapeDtypeStruct((groups, balanced), I32)] * 2,
        compiler_params=params(60 * 2**20),
        cost_estimate=cost(2 * 3 * half * capacity * width, 2 * capacity * width * 2),
    )(place, handoff, slots, counts, rows)


def masked_rank(product, tenant, first, rank):
    total = jnp.zeros((rank, product.shape[1]), F32)
    for label in range(product.shape[0] // rank):
        total = total + jnp.where(tenant == first + label, product[label * rank : (label + 1) * rank], 0.0)
    return total


def unpack(place, handoff, tenant, rows, arrived, down, rank, block):
    groups, balanced = tenant.shape
    capacity, width = rows.shape
    half = arrived[0].shape[0]

    def kernel(place_ref, handoff_ref, tenant_ref, rows_ref, *refs):
        arrived_refs = refs[: groups - 1]
        down_ref, gathered_ref, lowered_ref, turned = refs[groups - 1 :]
        step = pl.program_id(0)

        @pl.when(step == 0)
        def _():
            mine = place_ref[0]
            place_of = lax.broadcasted_iota(I32, (balanced, capacity), 0)
            here = lax.broadcasted_iota(I32, (balanced, capacity), 1)
            sent, got = before(handoff_ref, mine, mine, groups)
            inside = (place_of >= got) & (place_of < got + handoff_ref[mine, mine])
            pick = inside & (here == place_of - got + sent)
            total = jnp.dot(pick.astype(F32).astype(BF), rows_ref[...], preferred_element_type=F32)
            place_of = lax.broadcasted_iota(I32, (balanced, half), 0)
            here = lax.broadcasted_iota(I32, (balanced, half), 1)
            for k in range(1, groups):
                giver = mine ^ k
                _, got = before(handoff_ref, giver, mine, groups)
                inside = (place_of >= got) & (place_of < got + handoff_ref[giver, mine])
                pick = inside & (here == place_of - got)
                total = total + jnp.dot(
                    pick.astype(F32).astype(BF), arrived_refs[k - 1][...], preferred_element_type=F32
                )
            gathered_ref[...] = total.astype(BF)
            turned[...] = total.T.astype(BF)
            lowered_ref[...] = jnp.zeros_like(lowered_ref)

        product = jnp.dot(down_ref[...], turned[...], preferred_element_type=F32)
        lowered_ref[...] += masked_rank(product, tenant_ref[0:1, :], step * (block // rank), rank)

    return pl.pallas_call(
        kernel,
        grid=(down.shape[0] // block,),
        in_specs=[SMEM(), SMEM(), whole((groups, balanced)), whole((capacity, width))]
        + [whole((half, width))] * (groups - 1)
        + [pl.BlockSpec((block, width), lambda i: (i, 0))],
        out_specs=[whole((balanced, width)), whole((rank, balanced))],
        out_shape=[
            jax.ShapeDtypeStruct((balanced, width), BF),
            jax.ShapeDtypeStruct((rank, balanced), F32),
        ],
        scratch_shapes=[pltpu.VMEM((width, balanced), BF)],
        compiler_params=params(),
        cost_estimate=cost(2 * balanced * down.size, 2 * down.size + 6 * balanced * width),
    )(place, handoff, tenant, rows, *arrived, down)


def rank_backward(tenant, turned, up, lowered, block):
    rank, balanced = lowered.shape
    hidden = up.shape[1]
    steps = up.shape[0] // block

    def kernel(tenant_ref, turned_ref, lowered_ref, up_ref, out_ref, total_ref):
        step = pl.program_id(0)

        @pl.when(step == 0)
        def _():
            total_ref[:rank, :] = lowered_ref[...]
            total_ref[rank:, :] = jnp.zeros((rank, balanced), F32)

        product = jnp.dot(up_ref[...], turned_ref[...], preferred_element_type=F32)
        total_ref[rank:, :] += masked_rank(product, tenant_ref[0:1, :], step * (block // rank), rank)

        @pl.when(step == steps - 1)
        def _():
            out_ref[...] = total_ref[...].T

    return pl.pallas_call(
        kernel,
        grid=(steps,),
        in_specs=[
            whole(tenant.shape), whole(turned.shape), whole(lowered.shape),
            pl.BlockSpec((block, hidden), lambda i: (i, 0)),
        ],
        out_specs=whole((balanced, 2 * rank)),
        out_shape=jax.ShapeDtypeStruct((balanced, 2 * rank), F32),
        scratch_shapes=[pltpu.VMEM((2 * rank, balanced), F32)],
        compiler_params=params(50 * 2**20),
        cost_estimate=cost(2 * balanced * up.size, 2 * up.size),
    )(tenant, turned, lowered, up)


def base_gradient(owner, turned, weight, width, block, arrived=None):
    hidden, balanced = turned.shape
    steps = width // block

    def kernel(owner_ref, turned_ref, weight_ref, *refs):
        product = jnp.dot(weight_ref[...], turned_ref[...], preferred_element_type=F32).T
        if arrived is not None:
            product = product + refs[0][...].astype(F32)
        refs[-1][...] = product.astype(BF)

    piece = pl.BlockSpec((balanced, block), lambda i, owner_ref: (0, i))
    return pl.pallas_call(
        kernel,
        grid_spec=pltpu.PrefetchScalarGridSpec(
            num_scalar_prefetch=1,
            grid=(steps,),
            in_specs=[
                whole(turned.shape),
                pl.BlockSpec((block, hidden), lambda i, owner_ref: (owner_ref[0] * steps + i, 0)),
            ]
            + ([] if arrived is None else [piece]),
            out_specs=piece,
        ),
        out_shape=jax.ShapeDtypeStruct((balanced, width), BF),
        compiler_params=params(),
        cost_estimate=cost(2 * balanced * width * hidden, 2 * width * hidden),
    )(owner, turned, weight, *(() if arrived is None else (arrived,)))


def turn_and_far(owner, cotangent, weight, width, block):
    balanced, hidden = cotangent.shape
    steps = width // block

    def kernel(owner_ref, cotangent_ref, weight_ref, far_ref, turned_ref):
        @pl.when(pl.program_id(0) == 0)
        def _():
            turned_ref[...] = cotangent_ref[...].astype(F32).T.astype(BF)

        far_ref[...] = jnp.dot(weight_ref[...], turned_ref[...], preferred_element_type=F32).T.astype(BF)

    return pl.pallas_call(
        kernel,
        grid_spec=pltpu.PrefetchScalarGridSpec(
            num_scalar_prefetch=1,
            grid=(steps,),
            in_specs=[
                whole(cotangent.shape),
                pl.BlockSpec((block, hidden), lambda i, o: (o[0] * steps + i, 0)),
            ],
            out_specs=[pl.BlockSpec((balanced, block), lambda i, o: (0, i)), whole((hidden, balanced))],
        ),
        out_shape=[
            jax.ShapeDtypeStruct((balanced, width), BF),
            jax.ShapeDtypeStruct((hidden, balanced), BF),
        ],
        compiler_params=params(),
        cost_estimate=cost(2 * balanced * width * hidden, 2 * width * hidden),
    )(owner, cotangent, weight)


def spread(wide_ref, tenant_ref, ranks_ref, second, scale, tenants, rank):
    balanced, lanes = ranks_ref.shape
    vectors = scale * ranks_ref[...].astype(F32)
    turned = pltpu.roll(vectors, rank, 1)
    high = lax.broadcasted_iota(I32, (balanced, lanes), 1) >= rank
    twice = jnp.where(high, vectors, turned) if second else jnp.where(high, turned, vectors)
    half = (lax.broadcasted_iota(I32, (lanes, balanced), 0) >= rank).astype(F32)
    label = (tenant_ref[0:1, :].astype(F32) - half).T
    for pair in range(tenants // 2):
        wide_ref[:, pair * lanes : (pair + 1) * lanes] = jnp.where(label == 2.0 * pair, twice, 0.0).astype(BF)


def own_and_forward(owner, part, turned, weight, block):
    balanced, width = part.shape
    hidden = weight.shape[1]
    steps = width // block

    def kernel(owner_ref, part_ref, turned_ref, weight_ref, total_ref, own_ref):
        own_ref[...] = jnp.dot(weight_ref[...], turned_ref[...], preferred_element_type=F32).T.astype(BF)
        piece = jnp.dot(part_ref[...], weight_ref[...], preferred_element_type=F32)

        @pl.when(pl.program_id(0) == 0)
        def _():
            total_ref[...] = piece

        @pl.when(pl.program_id(0) > 0)
        def _():
            total_ref[...] += piece

    columns = pl.BlockSpec((balanced, block), lambda i, o: (0, i))
    return pl.pallas_call(
        kernel,
        grid_spec=pltpu.PrefetchScalarGridSpec(
            num_scalar_prefetch=1,
            grid=(steps,),
            in_specs=[
                columns,
                whole(turned.shape),
                pl.BlockSpec((block, hidden), lambda i, o: (o[0] * steps + i, 0)),
            ],
            out_specs=[whole((balanced, hidden)), columns],
        ),
        out_shape=[
            jax.ShapeDtypeStruct((balanced, hidden), F32),
            jax.ShapeDtypeStruct((balanced, width), BF),
        ],
        compiler_params=params(),
        cost_estimate=cost(4 * balanced * width * hidden, 2 * width * hidden),
    )(owner, part, turned, weight)


def forward(owners, parts, weight, block, total=None, tenant=None, ranks=None, up=None):
    balanced, width = parts[0].shape
    hidden = weight.shape[1]
    count = len(parts)
    last = up is not None

    def kernel(owners_ref, *refs):
        part_refs, weight_refs = refs[:count], refs[count : 2 * count]
        rest = list(refs[2 * count :])
        value = jnp.dot(part_refs[0][...], weight_refs[0][...], preferred_element_type=F32)
        for i in range(1, count):
            value = value + jnp.dot(part_refs[i][...], weight_refs[i][...], preferred_element_type=F32)
        if total is not None:
            value = value + rest.pop(0)[...]
        if last:
            tenant_ref, ranks_ref, up_ref = rest.pop(0), rest.pop(0), rest.pop(0)
            wide_ref = rest.pop()

            @pl.when(pl.program_id(0) == 0)
            def _():
                rank = ranks.shape[1] // 2
                spread(wide_ref, tenant_ref, ranks_ref, False, adapter_scale, up.shape[0] // rank, rank)

            value = value + jnp.dot(wide_ref[...], up_ref[...], preferred_element_type=F32)
        rest[0][...] = value.astype(rest[0].dtype)

    piece = pl.BlockSpec((balanced, block), lambda i, o: (0, i))
    in_specs = [whole((balanced, width))] * count
    for i in range(count):
        in_specs.append(pl.BlockSpec((width, block), lambda n, o, i=i: (o[i], n)))
    operands = [*parts, *([weight] * count)]
    if total is not None:
        in_specs.append(piece)
        operands.append(total)
    if last:
        in_specs += [whole(tenant.shape), whole(ranks.shape), pl.BlockSpec((up.shape[0], block), lambda i, o: (0, i))]
        operands += [tenant, ranks, up]
    return pl.pallas_call(
        kernel,
        grid_spec=pltpu.PrefetchScalarGridSpec(
            num_scalar_prefetch=1,
            grid=(hidden // block,),
            in_specs=in_specs,
            out_specs=piece,
            scratch_shapes=[pltpu.VMEM((balanced, up.shape[0]), BF)] if last else [],
        ),
        out_shape=jax.ShapeDtypeStruct((balanced, hidden), BF if last else F32),
        compiler_params=params(50 * 2**20 if last else VMEM_LIMIT),
        cost_estimate=cost(
            2 * balanced * hidden * (count * width + (up.shape[0] if last else 0)),
            2 * hidden * (count * width + (up.shape[0] if last else 0)),
        ),
    )(owners, *operands)


def finish_gradient(terms, tenant, ranks, down, block):
    balanced, width = terms[0].shape

    lanes = ranks.shape[1]
    rank = lanes // 2

    def kernel(tenant_ref, ranks_ref, down_ref, *refs):
        term_refs, out_ref, wide_ref = refs[:-2], refs[-2], refs[-1]
        spread(wide_ref, tenant_ref, ranks_ref, True, 1.0, down.shape[0] // rank, rank)
        for start in range(0, width, block):
            at = pl.ds(start, block)
            value = jnp.dot(wide_ref[...], down_ref[:, at], preferred_element_type=F32)
            for term_ref in term_refs:
                value = value + term_ref[:, at].astype(F32)
            out_ref[:, at] = value.astype(BF)
        out_ref[:, pl.ds(width, lanes)] = ranks_ref[...]

    return pl.pallas_call(
        kernel,
        grid=(1,),
        in_specs=[whole(tenant.shape), whole(ranks.shape), whole(down.shape)] + [whole((balanced, width))] * len(terms),
        out_specs=whole((balanced, width + lanes)),
        out_shape=jax.ShapeDtypeStruct((balanced, width + lanes), BF),
        scratch_shapes=[pltpu.VMEM((balanced, down.shape[0]), BF)],
        compiler_params=params(),
        cost_estimate=cost(2 * balanced * down.size, 2 * down.size),
    )(tenant, ranks, down, *terms)


def owned_gradient(place, slot, bundles, second, values, share, lanes, scale, block):
    groups, balanced = slot.shape
    rank = lanes // 2
    width = values[0].shape[1]
    column = bundles[0].shape[1] // lanes - 1

    def kernel(place_ref, slot_ref, *refs):
        rank_refs, value_refs = refs[:groups], refs[groups : 2 * groups]
        out_ref, wide_ref = refs[2 * groups :]

        @pl.when(pl.program_id(0) == 0)
        def _():
            first = place_ref[0] * share
            for k in range(groups):
                turned = rank_refs[k][...].astype(F32).T
                mine = turned[rank:, :] if second else turned[:rank, :]
                for s in range(share):
                    wide_ref[k, s * rank : (s + 1) * rank, :] = jnp.where(
                        slot_ref[k : k + 1, :] == first + s, mine, 0.0
                    ).astype(BF)

        value = jnp.dot(wide_ref[0], value_refs[0][...], preferred_element_type=F32)
        for k in range(1, groups):
            value = value + jnp.dot(wide_ref[k], value_refs[k][...], preferred_element_type=F32)
        out_ref[...] = (scale * value).astype(BF)

    return pl.pallas_call(
        kernel,
        grid=(width // block,),
        in_specs=[SMEM(), whole(slot.shape)]
        + [pl.BlockSpec((balanced, lanes), lambda i: (0, column))] * groups
        + [pl.BlockSpec((balanced, block), lambda i: (0, i))] * groups,
        out_specs=pl.BlockSpec((share * rank, block), lambda i: (0, i)),
        out_shape=jax.ShapeDtypeStruct((share * rank, width), BF),
        scratch_shapes=[pltpu.VMEM((groups, share * rank, balanced), BF)],
        compiler_params=params(),
        cost_estimate=cost(2 * groups * balanced * share * rank * width, 2 * width * (groups * balanced + share * rank)),
    )(place, slot, *bundles, *values)


def bring_home(place, handoff, bundles, capacity, width):
    balanced = bundles[0].shape[0]
    groups = handoff.shape[0]

    def kernel(place_ref, handoff_ref, *refs):
        out_ref = refs[-1]
        mine = place_ref[0]
        row = lax.broadcasted_iota(I32, (capacity, balanced), 0)
        here = lax.broadcasted_iota(I32, (capacity, balanced), 1)
        total = jnp.zeros((capacity, width), F32)
        for k in range(groups):
            taker = mine ^ k
            sent, got = before(handoff_ref, mine, taker, groups)
            inside = (row >= sent) & (row < sent + handoff_ref[mine, taker])
            pick = inside & (here == row - sent + got)
            total = total + jnp.dot(pick.astype(F32).astype(BF), refs[k][...], preferred_element_type=F32)
        out_ref[...] = total.astype(BF)

    return pl.pallas_call(
        kernel,
        grid=(1,),
        in_specs=[SMEM(), SMEM()] + [whole((balanced, width))] * groups,
        out_specs=whole((capacity, width)),
        out_shape=jax.ShapeDtypeStruct((capacity, width), BF),
        compiler_params=params(),
        cost_estimate=cost(2 * groups * balanced * capacity * width, 4 * groups * balanced * width),
    )(place, handoff, *bundles)


def swap(values, axis, distance):
    size = lax.axis_size(axis)
    return lax.ppermute(values, axis, [(i, i ^ distance) for i in range(size)])


def after(values, *earlier):
    return lax.optimization_barrier((values, *earlier))[0]


def fast_body(
    input_rows,
    cotangent,
    frozen_weight,
    adapter_down_weight,
    adapter_up_weight,
    tenant_row_counts,
    handoff_counts,
    tenant_gradient_slot,
):
    mine = lax.axis_index("dp")
    z = lax.axis_index("fsdp")
    balanced = cotangent.shape[0]
    capacity, width = input_rows.shape
    tenants, rank, hidden = adapter_up_weight.shape
    share = tenants // lax.axis_size("dp")
    place = mine.astype(I32).reshape(1)
    owner = [(z ^ k).astype(I32) for k in range(4)]
    down = adapter_down_weight.transpose(0, 2, 1).reshape(tenants * rank, width)
    up = adapter_up_weight.reshape(tenants * rank, hidden)

    *outgoing, tenant, slot = pack(
        place, handoff_counts, tenant_row_counts, tenant_gradient_slot, input_rows, balanced, balanced // 2
    )
    arrived = [None] * 3
    for k in (2, 3, 1):
        arrived[k - 1] = swap(outgoing[k - 1], "dp", k)
    far, turned = turn_and_far(
        owner[3].reshape(1), cotangent, after(frozen_weight, tenant), width, 512
    )
    for_far = swap(far, "fsdp", 1)
    near = base_gradient(owner[1].reshape(1), turned, after(frozen_weight, far), width, 512)
    from_near = swap(near, "fsdp", 1)
    gathered, lowered = unpack(
        place, handoff_counts, tenant, input_rows, arrived, after(down, near, *arrived), rank, 512
    )
    beside = swap(gathered, "fsdp", 1)
    pair = swap(gathered, "fsdp", 2)
    cot_x = swap(after(cotangent, *arrived, far), "dp", 2)
    across = base_gradient(owner[2].reshape(1), turned, after(frozen_weight, gathered), width, 512, for_far)
    from_pair = swap(across, "fsdp", 2)
    partial = rank_backward(tenant, turned, after(up, across), lowered, 512)
    first, own = own_and_forward(
        owner[0].reshape(1), gathered, turned, after(frozen_weight, partial, from_near), 512
    )
    late = after(partial, first, cot_x, beside)
    sums = [swap(late, "fsdp", k) for k in (1, 2, 3)]
    diagonal = swap(after(pair, first), "fsdp", 1)
    gathered_x = swap(after(gathered, first, cot_x), "dp", 2)
    second = forward(
        jnp.stack([owner[1], owner[2]]), [beside, pair], after(frozen_weight, first), 1024, first
    )
    scale = jnp.where(jnp.arange(2 * rank) < rank, 1.0, adapter_scale).astype(F32)
    ranks = ((after(partial, second, from_pair) + sums[0] + (sums[1] + sums[2])) * scale).astype(BF)
    bundle = finish_gradient([own, from_near, from_pair], tenant, ranks, after(down, second, diagonal), 512)
    bundle_x = swap(bundle, "dp", 2)
    bundle_c = swap(bundle, "dp", 1)
    cot_all = [
        cotangent,
        swap(after(cotangent, bundle), "dp", 1),
        cot_x,
        swap(after(cot_x, bundle), "dp", 1),
    ]
    outputs = forward(
        owner[3].reshape(1), [diagonal], after(frozen_weight, bundle), 1024, second, tenant, ranks, up
    )
    bundles = [bundle, bundle_c, bundle_x, swap(after(bundle_x, outputs), "dp", 1)]
    grad_b = owned_gradient(
        place, slot, after(bundles, outputs), False, cot_all, share, 2 * rank, adapter_scale, 2048
    )
    row_grad = bring_home(place, handoff_counts, after(bundles, grad_b), capacity, width)
    gathered_all = [
        gathered,
        swap(after(gathered, outputs), "dp", 1),
        gathered_x,
        swap(after(gathered_x, row_grad), "dp", 1),
    ]
    grad_a = owned_gradient(
        place, slot, after(bundles, row_grad), True, gathered_all, share, 2 * rank, 1.0, 768
    )
    return (
        outputs,
        row_grad,
        grad_a.reshape(share, rank, width).transpose(0, 2, 1),
        grad_b.reshape(share, rank, hidden),
    )


def solution(mesh):
    placed = (
        P(("groups", "dp"), "fsdp"),
        P(("groups", "dp"), "fsdp"),
        P(None, "fsdp"),
        P("groups", "fsdp", None),
        P("groups", None, "fsdp"),
        P("groups", None),
        P("groups", None),
        P("groups"),
    )
    four_by_four = mesh.shape["dp"] == 4 and mesh.shape["fsdp"] == 4
    return jax.shard_map(
        fast_body if four_by_four else plain_body,
        mesh=mesh,
        in_specs=placed,
        out_specs=(
            P(("groups", "dp"), "fsdp"),
            P(("groups", "dp"), "fsdp"),
            P(("groups", "dp"), "fsdp", None),
            P(("groups", "dp"), None, "fsdp"),
        ),
        check_vma=False,
    )
```
